256 devices in a mesh: leaf: 16 (over z, x_lo), seq: 16 (over x_hi, y, core).
Axes of the slice: x: 4 (x_hi: 2, x_lo: 2; x = x_hi * 2 + x_lo), y: 4, z: 8, core: 2. Of those that a mesh axis runs over, the one named last changes fastest.
Arguments:
- query_raw: bfloat16 [16, 5120, 2048], P('leaf', 'seq'), may hold values from -6 to 6
- key_raw: bfloat16 [16, 5120, 512], P('leaf', 'seq'), may hold values from -6 to 6
- value_raw: bfloat16 [16, 5120, 512], P('leaf', 'seq'), may hold values from -6 to 6
- grad_out: bfloat16 [16, 5120, 2048], P('leaf', 'seq'), may hold values from -6 to 6
- query_gain: float32 [128], replicated, may hold values from 0.5 to 1.5
- key_gain: float32 [128], replicated, may hold values from 0.5 to 1.5
- leaf_parent: int32 [16, 16], P('leaf', 'seq'), may hold values from 0 to 3
- leaf_blocks: int32 [16, 16], P('leaf', 'seq'), may hold values from 1 to 3, as said below
Outputs:
- grad_query: bfloat16 [16, 5120, 2048], P('leaf', 'seq')
- grad_key: bfloat16 [16, 5120, 512], P('leaf', 'seq')
- grad_value: bfloat16 [16, 5120, 512], P('leaf', 'seq')
- query_gain_grad: float32 [128], replicated
- key_gain_grad: float32 [128], replicated
The draws below stay inside these ranges and needn't reach their ends.
Inputs may be any that keep to these rules, and one draw needn't show every extreme that they name: `leaf_blocks`: in every tree some leaf has all 3 blocks.
All inputs are finite; a program needn't handle non-finite values.
Results may differ from the reference program's by a relative error of at most 0.011.
Values may be sent and summed in bfloat16 or wider, within the bound.
A program may use at most 128 MiB of HBM per device.

```python
import jax
import jax.numpy as jnp
from jax import lax

HQ = 16
HK = 4
DH = 128
R_DEV = 64
B_DEV = 64
LEAF_BLOCK = 64
LEAF_BLOCKS = 3
GROUP = 4
L_DEV = 192
ROWS = 320
TREES = 16
BRANCHES = 4
TOKENS = 5120
N_SEQ = 16


def draw_leaf_blocks(key, part):
    key = jax.random.fold_in(key, 11)
    key_counts, key_choice = jax.random.split(key)
    counts = jax.random.randint(key_counts, (TREES, N_SEQ), 1, LEAF_BLOCKS + 1)
    chosen = jax.random.randint(key_choice, (TREES, 1), 0, N_SEQ)
    longest = jnp.arange(N_SEQ)[None, :] == chosen
    return jnp.where(longest, LEAF_BLOCKS, counts).astype(jnp.int32)


def touch_ends(result, own_key, least, largest):
    longest = result.shape.index(max(result.shape))
    spots = []
    for shift in (0, 1):
        where = [jax.random.randint(jax.random.fold_in(own_key, axis), (), 0, length) for axis, length in enumerate(result.shape)]
        where[longest] = (where[longest] + shift) % result.shape[longest]
        spots.append(tuple(where))
    return result.at[spots[0]].set(least).at[spots[1]].set(largest)


def levels(stream_key, shape, pieces, least, top_value):
    loudness, own = 1.0, jax.random.fold_in(stream_key, 6)
    for dim, shards_of in pieces:
        draws = jnp.exp(jax.random.uniform(jax.random.fold_in(own, dim), (shards_of,), jnp.float32, least / len(pieces), top_value / len(pieces)))
        loudness = loudness * jnp.repeat(draws, shape[dim] // shards_of).reshape([-1 if axis == dim else 1 for axis in range(len(shape))])
    return loudness


def centred(stream_key, shape, scale, most, shards=(), kind=jnp.bfloat16):
    level = levels(stream_key, shape, shards, -0.22, 0.18) if shards else 1.0
    values = jax.random.normal(stream_key, shape, jnp.float32) * scale * level
    return jnp.minimum(jnp.maximum(values, -most), most).astype(kind)


def setup_inputs(seed: int = 0) -> dict:
    arg_keys = jax.random.split(jax.random.key(seed), 9)
    return {
        "query_raw": centred(arg_keys[0], (TREES, TOKENS, HQ * DH), 1.0, 6.0, ((0, 16), (1, 16))),
        "key_raw": centred(arg_keys[1], (TREES, TOKENS, HK * DH), 1.0, 6.0, ((0, 16), (1, 16))),
        "value_raw": centred(arg_keys[2], (TREES, TOKENS, HK * DH), 1.0, 6.0, ((0, 16), (1, 16))),
        "grad_out": centred(arg_keys[3], (TREES, TOKENS, HQ * DH), 1.0, 6.0, ((0, 16), (1, 16))),
        "query_gain": jnp.clip(1.0 + 0.1 * jax.random.normal(arg_keys[4], (DH,), jnp.float32), 0.5, 1.5),
        "key_gain": jnp.clip(1.0 + 0.1 * jax.random.normal(arg_keys[5], (DH,), jnp.float32), 0.5, 1.5),
        "leaf_parent": touch_ends(jax.random.randint(arg_keys[6], (TREES, N_SEQ), 0, BRANCHES), jax.random.fold_in(arg_keys[6], 1), 0, BRANCHES - 1).astype(jnp.int32),
        "leaf_blocks": draw_leaf_blocks(jax.random.fold_in(arg_keys[8], 71), 0),
    }


EPS = 1e-06

def contract(form, left, right):
    return jnp.einsum(form, left.astype(jnp.float32), right.astype(jnp.float32))

def normalize(raw, gain):
    values = raw.astype(jnp.float32)
    inverse = lax.rsqrt(lax.optimization_barrier(jnp.mean(values * values, axis=-1, keepdims=True)) + EPS)
    return ((values * inverse * gain).astype(jnp.bfloat16), inverse)

def norm_backward(raw, inverse, gain, upstream):
    values = raw.astype(jnp.float32)
    scaled = upstream * gain
    grad_raw = inverse * scaled - values * inverse * inverse * inverse * lax.optimization_barrier(jnp.mean(scaled * values, axis=-1, keepdims=True))
    grad_gain = lax.optimization_barrier(jnp.sum((upstream * values * inverse).reshape(-1, values.shape[-1]), axis=0))
    return (grad_raw.astype(jnp.bfloat16), grad_gain)

def query_major(flat, kv_heads, head_dim):
    return flat.reshape(flat.shape[0], kv_heads, -1, head_dim).transpose(1, 0, 2, 3)

def key_major(flat, kv_heads, head_dim):
    return flat.reshape(flat.shape[0], kv_heads, head_dim).transpose(1, 0, 2)

def key_flat(major):
    return major.transpose(1, 0, 2).reshape(major.shape[1], -1)

def query_flat(major):
    return major.transpose(1, 0, 2, 3).reshape(major.shape[1], -1)

def forward_terms(query, keys, values, allowed):
    scale = query.shape[-1] ** (-0.5)
    scores = contract('qgd,jd->gqj', query, keys) * scale
    expos = jnp.where(allowed[None], jnp.exp(scores), 0.0)
    total = lax.optimization_barrier(jnp.sum(expos, axis=-1))
    weighted = contract('gqj,jd->qgd', expos.astype(jnp.bfloat16), values)
    return (total, weighted)

def backward_terms(query, keys, values, upstream, allowed, total, dot_row):
    scale = query.shape[-1] ** (-0.5)
    scores = contract('qgd,jd->gqj', query, keys) * scale
    probs = jnp.where(allowed[None], jnp.exp(scores), 0.0) / total[:, :, None]
    grad_probs = contract('qgd,jd->gqj', upstream, values)
    grad_scores = (probs * (grad_probs - dot_row[:, :, None])).astype(jnp.bfloat16)
    grad_query = contract('gqj,jd->qgd', grad_scores, keys) * scale
    grad_keys = contract('gqj,qgd->jd', grad_scores, query) * scale
    grad_values = contract('gqj,qgd->jd', probs.astype(jnp.bfloat16), upstream)
    return (grad_query, grad_keys, grad_values)

def set_forward(query_h, keys_h, values_h, allowed):

    def one_head(bundle):
        return forward_terms(bundle[0], bundle[1], bundle[2], allowed)
    return lax.map(one_head, (query_h, keys_h, values_h))

def set_backward(query_h, keys_h, values_h, upstream_h, allowed, total_h, dot_h):

    def one_head(bundle):
        return backward_terms(bundle[0], bundle[1], bundle[2], bundle[3], allowed, bundle[4], bundle[5])
    return lax.map(one_head, (query_h, keys_h, values_h, upstream_h, total_h, dot_h))

def root_forward(query_h, piece_keys, piece_values, limit, start, kv_heads, head_dim):
    span = piece_keys.shape[0]
    allowed = (start + jnp.arange(span, dtype=jnp.int32))[None, :] < limit[:, None]
    return set_forward(query_h, key_major(piece_keys, kv_heads, head_dim), key_major(piece_values, kv_heads, head_dim), allowed)

def root_backward(query_h, upstream_h, piece_keys, piece_values, limit, start, total, dot_h, kv_heads, head_dim):
    span = piece_keys.shape[0]
    allowed = (start + jnp.arange(span, dtype=jnp.int32))[None, :] < limit[:, None]
    grad_query, grad_keys, grad_values = set_backward(query_h, key_major(piece_keys, kv_heads, head_dim), key_major(piece_values, kv_heads, head_dim), upstream_h, allowed, total, dot_h)
    return (grad_query, key_flat(grad_keys), key_flat(grad_values))

def side_sets(device_index, parent, leaf_length, keys_loc, values_loc, branch_keys, branch_values, kv_heads, head_dim):
    span = GROUP * B_DEV
    own_start = (device_index // GROUP * span).astype(jnp.int32)
    parent_start = (parent * span).astype(jnp.int32)
    own_query = device_index % GROUP * B_DEV + jnp.arange(B_DEV, dtype=jnp.int32)
    key_ids = jnp.arange(span, dtype=jnp.int32)
    own_allowed = key_ids[None, :] <= own_query[:, None]
    leaf_ids = jnp.arange(L_DEV, dtype=jnp.int32)
    leaf_allowed = (leaf_ids[None, :] <= leaf_ids[:, None]) & (leaf_ids[None, :] < leaf_length)
    parent_allowed = jnp.zeros((L_DEV, span), jnp.int32) == 0

    def heads(flat):
        return key_major(flat, kv_heads, head_dim)
    own_set = (R_DEV, B_DEV, heads(lax.dynamic_slice_in_dim(branch_keys, own_start, span, 0)), heads(lax.dynamic_slice_in_dim(branch_values, own_start, span, 0)), own_allowed)
    parent_set = (R_DEV + B_DEV, L_DEV, heads(lax.dynamic_slice_in_dim(branch_keys, parent_start, span, 0)), heads(lax.dynamic_slice_in_dim(branch_values, parent_start, span, 0)), parent_allowed)
    leaf_set = (R_DEV + B_DEV, L_DEV, heads(keys_loc[R_DEV + B_DEV:]), heads(values_loc[R_DEV + B_DEV:]), leaf_allowed)
    return ([own_set, parent_set, leaf_set], own_start, parent_start)

def add_sides_forward(query_h, total, weighted, sets):
    for row_start, count, keys_h, values_h, allowed in sets:
        row_stop = row_start + count
        part_total, part_weighted = set_forward(query_h[:, row_start:row_stop], keys_h, values_h, allowed)
        total = total.at[:, :, row_start:row_stop].add(part_total)
        weighted = weighted.at[:, row_start:row_stop].add(part_weighted)
    return (total, weighted)

def dot_rows(upstream_h, weighted, total):
    output = weighted / jnp.transpose(total, (0, 2, 1))[..., None]
    return jnp.transpose(lax.optimization_barrier(jnp.sum(upstream_h.astype(jnp.float32) * output, axis=-1)), (0, 2, 1))

def add_sides_backward(query_h, upstream_h, total, dot_h, grad_q, sets):
    key_grads = []
    for row_start, count, keys_h, values_h, allowed in sets:
        row_stop = row_start + count
        part_q, part_k, part_v = set_backward(query_h[:, row_start:row_stop], keys_h, values_h, upstream_h[:, row_start:row_stop], allowed, total[:, :, row_start:row_stop], dot_h[:, :, row_start:row_stop])
        grad_q = grad_q.at[:, row_start:row_stop].add(part_q)
        key_grads.append((key_flat(part_k), key_flat(part_v)))
    return (grad_q, key_grads)

def branch_partials(key_grads, own_start, parent_start, total_rows, width):
    grad_k = jnp.zeros((total_rows, width), jnp.float32)
    grad_v = jnp.zeros((total_rows, width), jnp.float32)
    for grads, offset in zip(key_grads[:2], (own_start, parent_start)):
        span = grads[0].shape[0]
        grad_k = lax.dynamic_update_slice_in_dim(grad_k, lax.dynamic_slice_in_dim(grad_k, offset, span, 0) + grads[0], offset, 0)
        grad_v = lax.dynamic_update_slice_in_dim(grad_v, lax.dynamic_slice_in_dim(grad_v, offset, span, 0) + grads[1], offset, 0)
    return (grad_k, grad_v)

def device_pass(device_index, query_n, upstream, keys_loc, values_loc, parent, blocks, root_keys, root_values, branch_keys, branch_values):
    row_count = query_n.shape[0]
    row_ids = jnp.arange(row_count, dtype=jnp.int32)
    root_total = root_keys.shape[0]
    limit = jnp.where(row_ids < R_DEV, device_index * R_DEV + row_ids + 1, root_total).astype(jnp.int32)
    leaf_length = blocks * LEAF_BLOCK
    valid = (row_ids < R_DEV + B_DEV) | (row_ids - R_DEV - B_DEV < leaf_length)
    upstream = jnp.where(valid[:, None], upstream, jnp.zeros_like(upstream))
    query_h = query_major(query_n, HK, DH)
    upstream_h = query_major(upstream, HK, DH)
    sets, own_start, parent_start = side_sets(device_index, parent, leaf_length, keys_loc, values_loc, branch_keys, branch_values, HK, DH)
    root_tot, root_weighted = root_forward(query_h, root_keys, root_values, limit, 0, HK, DH)
    total, weighted = add_sides_forward(query_h, root_tot, root_weighted, sets)
    dot_h = dot_rows(upstream_h, weighted, total)
    grad_q, root_gk, root_gv = root_backward(query_h, upstream_h, root_keys, root_values, limit, 0, total, dot_h, HK, DH)
    grad_q, key_grads = add_sides_backward(query_h, upstream_h, total, dot_h, grad_q, sets)
    branch_gk, branch_gv = branch_partials(key_grads, own_start, parent_start, branch_keys.shape[0], root_keys.shape[1])
    return (query_flat(grad_q), key_grads[2][0], key_grads[2][1], root_gk, root_gv, branch_gk, branch_gv)

def tree_pass(bundle, query_gain, key_gain):
    query_raw, key_raw, value_raw, grad_out, parents, blocks = bundle
    shaped_q = query_raw.reshape(N_SEQ, ROWS, HQ, DH)
    shaped_k = key_raw.reshape(N_SEQ, ROWS, HK, DH)
    query_n, query_inverse = normalize(shaped_q, query_gain)
    keys_n, keys_inverse = normalize(shaped_k, key_gain)
    query_n = query_n.reshape(N_SEQ, ROWS, -1)
    keys_n = keys_n.reshape(N_SEQ, ROWS, -1)
    values_all = value_raw.reshape(N_SEQ, ROWS, -1)
    width_kv = HK * DH
    root_keys = keys_n[:, :R_DEV].reshape(-1, width_kv)
    root_values = values_all[:, :R_DEV].reshape(-1, width_kv)
    branch_keys = keys_n[:, R_DEV:R_DEV + B_DEV].reshape(-1, width_kv)
    branch_values = values_all[:, R_DEV:R_DEV + B_DEV].reshape(-1, width_kv)

    def one_device(device_bundle):
        return device_pass(*device_bundle, root_keys, root_values, branch_keys, branch_values)
    results = lax.map(one_device, (jnp.arange(N_SEQ, dtype=jnp.int32), query_n, grad_out.reshape(N_SEQ, ROWS, -1), keys_n, values_all, parents, blocks))
    grad_q, leaf_gk, leaf_gv, root_gk, root_gv, branch_gk, branch_gv = results
    grad_keys = jnp.concatenate([lax.optimization_barrier(jnp.sum(root_gk, axis=0)).reshape(N_SEQ, R_DEV, -1), lax.optimization_barrier(jnp.sum(branch_gk, axis=0)).reshape(N_SEQ, B_DEV, -1), leaf_gk], axis=1)
    grad_values = jnp.concatenate([lax.optimization_barrier(jnp.sum(root_gv, axis=0)).reshape(N_SEQ, R_DEV, -1), lax.optimization_barrier(jnp.sum(branch_gv, axis=0)).reshape(N_SEQ, B_DEV, -1), leaf_gv], axis=1).astype(jnp.bfloat16)
    grad_query, query_gain_part = norm_backward(shaped_q, query_inverse, query_gain, grad_q.reshape(N_SEQ, ROWS, HQ, DH))
    grad_key, key_gain_part = norm_backward(shaped_k, keys_inverse, key_gain, grad_keys.reshape(N_SEQ, ROWS, HK, DH))
    return (grad_query.reshape(TOKENS, -1), grad_key.reshape(TOKENS, -1), grad_values.reshape(TOKENS, -1), query_gain_part, key_gain_part)

def reference(query_raw, key_raw, value_raw, grad_out, query_gain, key_gain, leaf_parent, leaf_blocks):

    def one_tree(bundle):
        return tree_pass(bundle, query_gain, key_gain)
    results = lax.map(one_tree, (query_raw, key_raw, value_raw, grad_out, leaf_parent, leaf_blocks))
    return (results[0], results[1], results[2], lax.optimization_barrier(jnp.sum(results[3], axis=0)), lax.optimization_barrier(jnp.sum(results[4], axis=0)))
```

```python
import functools
import math

import jax
import jax.numpy as jnp
from jax import lax
from jax.experimental import pallas as pl
from jax.experimental.pallas import tpu as pltpu
from jax.sharding import PartitionSpec as P

HQ = 16
HK = 4
DH = 128
GQ = HQ // HK
R_DEV = 64
B_DEV = 64
LEAF_BLOCK = 64
L_DEV = 192
ROWS = 320
N_SEQ = 16
N_ROOT = R_DEV * N_SEQ
SPAN = 256
RB = 256
Q_ROWS = ROWS * GQ
LEAF_AT = GQ * (R_DEV + B_DEV)
EPS = 1e-06
SCALE = 1.0 / math.sqrt(DH)
EXP2_SCALE = SCALE / math.log(2.0)

F32 = jnp.float32
BF16 = jnp.bfloat16
MESH = pl.DeviceIdType.MESH
NT = (((1,), (1,)), ((), ()))
NN = (((1,), (0,)), ((), ()))
TN = (((0,), (0,)), ((), ()))

SEGMENTS = ((0, R_DEV, 0), (R_DEV, B_DEV, GQ * R_DEV), (R_DEV + B_DEV, L_DEV, LEAF_AT))

G_X, G_UP_OWN, G_DN_OWN, G_UP_PAIR, G_DN_PAIR, G_UP_FAR, G_DN_FAR, G_CORE = range(8)
N_G = G_CORE + 8
R_CORE, R_UP_FAR, R_DN_FAR, R_UP, R_DN, R_X = range(6)
N_R = 6


def dot(left, right, dims):
    return lax.dot_general(left, right, dims, preferred_element_type=F32)


def inverse_norm(values):
    return lax.rsqrt(jnp.mean(values * values, axis=-1, keepdims=True) + EPS)


def norm_backward(values, inverse, gain, upstream):
    scaled = upstream * gain
    mean = jnp.mean(scaled * values, axis=-1, keepdims=True)
    return inverse * scaled - values * (inverse * inverse * inverse * mean)


def fold(array):
    return jnp.sum(array.reshape(array.shape[0] // 8, 8, array.shape[1]), axis=0)


def kernel(
    n_leaf,
    parent_ref,
    blocks_ref,
    q_ref,
    k_ref,
    v_ref,
    u_ref,
    qgain_ref,
    kgain_ref,
    gq_ref,
    gk_ref,
    gv_ref,
    gains_ref,
    kv,
    leaf_kv,
    side,
    qn,
    up,
    expo,
    gprobs,
    gscores,
    q_scaled,
    up_scaled,
    inv_rows,
    dot_rows,
    grad_qn,
    parts,
    from_core,
    from_far,
    from_near,
    to_x,
    kept,
    from_x,
    gain_part,
    gain_seq,
    gain_leaf,
    g_send,
    g_recv,
    r_send,
    r_recv,
    a_send,
    a_recv,
    b_send,
    b_recv,
):
    me = lax.axis_index("seq")
    me_leaf = lax.axis_index("leaf")
    x = me // 8
    y = (me // 2) % 4
    c = me % 2
    y_up, y_dn, y_far = (y + 1) % 4, (y + 3) % 4, (y + 2) % 4

    def place(px, py, pc):
        return px * 8 + py * 2 + pc

    dev_core = place(x, y, 1 - c)
    dev_x = place(1 - x, y, c)
    dev_up = place(x, y_up, c)
    dev_dn = place(x, y_dn, c)
    parent = parent_ref[0, 0]
    leaf_length = blocks_ref[0, 0] * LEAF_BLOCK
    own_branch = me // 4

    barrier = pltpu.get_barrier_semaphore()

    def greet_seq(step, carry):
        pl.semaphore_signal(
            barrier, inc=1, device_id=(me_leaf, (me + step) % N_SEQ), device_id_type=MESH
        )
        return carry

    def greet_leaf(step, carry):
        pl.semaphore_signal(
            barrier, inc=1, device_id=((me_leaf + step) % n_leaf, me), device_id_type=MESH
        )
        return carry

    lax.fori_loop(1, N_SEQ, greet_seq, 0)
    lax.fori_loop(1, n_leaf, greet_leaf, 0)

    kgain = kgain_ref[...]
    own_rows = pl.ds(pl.multiple_of(me * R_DEV, R_DEV), R_DEV)
    for h in range(HK):
        cols = slice(h * DH, (h + 1) * DH)
        raw = k_ref[:, cols].astype(F32)
        normed = (raw * inverse_norm(raw) * kgain).astype(BF16)
        values = v_ref[:, cols]
        kv[h, 0, 0, own_rows, :] = normed[:R_DEV]
        kv[h, 1, 0, own_rows, :] = normed[R_DEV : R_DEV + B_DEV]
        leaf_kv[h, 0] = normed[R_DEV + B_DEV :]
        kv[h, 0, 1, own_rows, :] = values[:R_DEV]
        kv[h, 1, 1, own_rows, :] = values[R_DEV : R_DEV + B_DEV]
        leaf_kv[h, 1] = values[R_DEV + B_DEV :]

    pl.semaphore_wait(barrier, N_SEQ - 1 + n_leaf - 1)

    def piece(h, owner):
        return kv.at[h, :, :, pl.ds(pl.multiple_of(owner * R_DEV, R_DEV), R_DEV), :]

    def g_copy(h, which, owner, target):
        return pltpu.make_async_remote_copy(
            src_ref=piece(h, owner),
            dst_ref=piece(h, owner),
            send_sem=g_send.at[h, which],
            recv_sem=g_recv.at[h, which],
            device_id=(me_leaf, target),
            device_id_type=MESH,
        )

    own, pair = me, dev_x
    ring = (
        own,
        pair,
        place(x, y_dn, c),
        place(x, y_up, c),
        place(1 - x, y_dn, c),
        place(1 - x, y_up, c),
        place(0, y_far, c),
        place(1, y_far, c),
    )
    core_ring = tuple(owner + 1 - 2 * c for owner in ring)

    def gather_a(h):
        g_copy(h, G_X, own, dev_x).start()
        g_copy(h, G_UP_OWN, own, dev_up).start()
        g_copy(h, G_DN_OWN, own, dev_dn).start()
        g_copy(h, G_CORE, own, dev_core).start()

    def gather_b(h):
        g_copy(h, G_X, pair, dev_x).wait_recv()
        g_copy(h, G_UP_PAIR, pair, dev_up).start()
        g_copy(h, G_DN_PAIR, pair, dev_dn).start()
        g_copy(h, G_CORE + 1, pair, dev_core).start()

    def gather_c(h):
        g_copy(h, G_UP_OWN, ring[2], dev_dn).wait_recv()
        g_copy(h, G_DN_OWN, ring[3], dev_up).wait_recv()
        g_copy(h, G_UP_PAIR, ring[4], dev_dn).wait_recv()
        g_copy(h, G_DN_PAIR, ring[5], dev_up).wait_recv()
        g_copy(h, G_UP_FAR, place(0, y_dn, c), dev_up).start()
        g_copy(h, G_DN_FAR, place(1, y_up, c), dev_dn).start()
        for n in range(2, 6):
            g_copy(h, G_CORE + n, ring[n], dev_core).start()

    def gather_d(h):
        g_copy(h, G_UP_FAR, ring[6], dev_dn).wait_recv()
        g_copy(h, G_DN_FAR, ring[7], dev_up).wait_recv()
        for n in range(6, 8):
            g_copy(h, G_CORE + n, ring[n], dev_core).start()

    def gather_e(h):
        for n in range(8):
            g_copy(h, G_CORE + n, core_ring[n], dev_core).wait_recv()

    def gather_sent(h):
        for n in range(N_G):
            g_copy(h, n, own, dev_core).wait_send()

    def r_copy(h, which, src, dst, target):
        return pltpu.make_async_remote_copy(
            src_ref=src,
            dst_ref=dst,
            send_sem=r_send.at[h, which],
            recv_sem=r_recv.at[h, which],
            device_id=(me_leaf, target),
            device_id_type=MESH,
        )

    def r_core(h):
        return r_copy(h, R_CORE, parts.at[h, 1 - c], from_core.at[h], dev_core)

    def r_far(h):
        return (
            r_copy(h, R_UP_FAR, parts.at[h, c, y_far, 0], from_far.at[h, 0], dev_up),
            r_copy(h, R_DN_FAR, parts.at[h, c, y_far, 1], from_far.at[h, 1], dev_dn),
        )

    def r_near(h):
        return (
            r_copy(h, R_UP, parts.at[h, c, y_up], from_near.at[h, 0], dev_up),
            r_copy(h, R_DN, parts.at[h, c, y_dn], from_near.at[h, 1], dev_dn),
        )

    def r_x(h):
        return r_copy(h, R_X, to_x.at[h], from_x.at[h], dev_x)

    def added(left, right):
        return left.astype(F32) + right.astype(F32)

    def reduce_a(h):
        r_core(h).wait_recv()
        for block in range(4):
            for side_x in range(2):
                parts[h, c, block, side_x] = added(
                    parts[h, c, block, side_x], from_core[h, block, side_x]
                ).astype(BF16)
        for copy in r_far(h):
            copy.start()

    def reduce_b(h):
        for copy in r_far(h):
            copy.wait_recv()
        parts[h, c, y_up, 0] = added(parts[h, c, y_up, 0], from_far[h, 0]).astype(BF16)
        parts[h, c, y_dn, 1] = added(parts[h, c, y_dn, 1], from_far[h, 1]).astype(BF16)
        for copy in r_near(h):
            copy.start()

    def reduce_c(h):
        for copy in r_near(h):
            copy.wait_recv()

        def total(side_x):
            return added(parts[h, c, y, side_x], from_near[h, 0, side_x]) + from_near[
                h, 1, side_x
            ].astype(F32)

        to_x[h] = total(1 - x).astype(BF16)
        r_x(h).start()
        kept[h] = total(x)

    def reduce_d(h):
        r_x(h).wait_recv()
        cols = pl.ds(pl.multiple_of(h * DH, DH), DH)
        for kind, start in ((0, 0), (1, R_DEV)):
            rows = slice(start, start + R_DEV)
            grad_kn = kept[h, kind, 0] + from_x[h, kind, 0].astype(F32)
            grad_v = kept[h, kind, 1] + from_x[h, kind, 1].astype(F32)
            raw = k_ref[rows, cols].astype(F32)
            gk_ref[rows, cols] = norm_backward(
                raw, inverse_norm(raw), kgain_ref[...], grad_kn
            ).astype(BF16)
            gv_ref[rows, cols] = grad_v.astype(BF16)

    def reduce_sent(h):
        r_core(h).wait_send()
        for copy in r_far(h) + r_near(h):
            copy.wait_send()
        r_x(h).wait_send()

    for h in range(HK):
        gather_a(h)

    def prepare(h):
        for start, count, at in SEGMENTS:
            for g in range(GQ):
                cols = pl.ds(pl.multiple_of(h * GQ * DH + g * DH, DH), DH)
                rows = slice(start, start + count)
                dst = slice(at + g * count, at + (g + 1) * count)
                raw = q_ref[rows, cols].astype(F32)
                qn[h, dst, :] = (raw * inverse_norm(raw) * qgain_ref[...]).astype(BF16)
                grads = u_ref[rows, cols]
                if start == R_DEV + B_DEV:
                    ids = lax.broadcasted_iota(jnp.int32, (count, DH), 0)
                    grads = jnp.where(ids < leaf_length, grads.astype(F32), 0.0).astype(BF16)
                up[h, dst, :] = grads

    prepare(0)
    gather_b(0)
    prepare(1)
    gather_c(0)
    prepare(2)
    gather_d(0)
    prepare(3)
    gather_e(0)
    gain_part[...] = jnp.zeros_like(gain_part)

    def one_head(h, carry):
        for t in range(2):
            picked = kv[h, 1, t, 0:SPAN, :]
            for b in range(1, 4):
                picked = lax.select_n(
                    parent == b, picked, kv[h, 1, t, b * SPAN : (b + 1) * SPAN, :]
                )
            side[t, 0:SPAN, :] = picked
            side[t, SPAN : SPAN + L_DEV, :] = leaf_kv[h, t]
            side[t, SPAN + L_DEV :, :] = kv[
                h, 1, t, pl.ds(pl.multiple_of(own_branch * SPAN, SPAN), SPAN), :
            ]

        def scores_of(rb):
            rows = slice(rb * RB, (rb + 1) * RB)
            queries = qn[h, rows, :]
            upstream = up[h, rows, :]

            def chunk(keys, values, dst, allowed):
                count = keys.shape[0]
                e = jnp.exp2(dot(keys, queries, NT) * EXP2_SCALE)
                if allowed is not None:
                    e = jnp.where(allowed, e, 0.0)
                gp = dot(values, upstream, NT)
                expo[dst : dst + count, rows] = e.astype(BF16)
                gprobs[dst : dst + count, rows] = gp
                return fold(e), fold(e * gp)

            def key_ids(count):
                return lax.broadcasted_iota(jnp.int32, (count, RB), 0)

            def row_ids(count, first, period):
                return (lax.broadcasted_iota(jnp.int32, (count, RB), 1) + first) % period

            found = []
            for n in range(N_ROOT // SPAN):
                keys = slice(n * SPAN, (n + 1) * SPAN)
                allowed = None
                if rb == 0:
                    allowed = key_ids(SPAN) + n * SPAN <= row_ids(SPAN, 0, R_DEV) + me * R_DEV
                found.append(chunk(kv[h, 0, 0, keys, :], kv[h, 0, 1, keys, :], n * SPAN, allowed))
            if rb == 1:
                allowed = key_ids(SPAN) <= row_ids(SPAN, 0, B_DEV) + (me % 4) * B_DEV
                own_keys = slice(SPAN + L_DEV, 2 * SPAN + L_DEV)
                found.append(chunk(side[0, own_keys, :], side[1, own_keys, :], N_ROOT, allowed))
            if rb >= 2:
                found.append(chunk(side[0, :SPAN, :], side[1, :SPAN, :], N_ROOT, None))
                ids = key_ids(L_DEV)
                allowed = (ids <= row_ids(L_DEV, (rb - 2) * RB, L_DEV)) & (ids < leaf_length)
                leaf_keys = slice(SPAN, SPAN + L_DEV)
                found.append(
                    chunk(side[0, leaf_keys, :], side[1, leaf_keys, :], N_ROOT + SPAN, allowed)
                )
            total = jnp.sum(sum(f[0] for f in found), axis=0, keepdims=True)
            weighted = jnp.sum(sum(f[1] for f in found), axis=0, keepdims=True)
            inverse = 1.0 / total
            dot_rows[:, rows] = jnp.broadcast_to(weighted * inverse, (8, RB))
            spread = jnp.transpose(jnp.broadcast_to(inverse, (DH, RB)))
            inv_rows[rows, :] = spread
            q_scaled[rows, :] = (queries.astype(F32) * (spread * SCALE)).astype(BF16)
            up_scaled[rows, :] = (upstream.astype(F32) * spread).astype(BF16)

        def key_grads(keys, rows):
            gs = (
                expo[keys, rows].astype(F32) * (gprobs[keys, rows] - dot_rows[0:1, rows])
            ).astype(BF16)
            gscores[keys, rows] = gs
            return (
                dot(gs, q_scaled[rows, :], NN),
                dot(expo[keys, rows], up_scaled[rows, :], NN),
            )

        def gain_term(grad_kn, keys):
            return fold(grad_kn * keys.astype(F32))

        def root_grads(n):
            keys = slice(n * SPAN, (n + 1) * SPAN)
            grads = key_grads(keys, slice(0, Q_ROWS))
            gain_part[0:8] += gain_term(grads[0], kv[h, 0, 0, keys, :])
            for q in range(4):
                owner = 4 * n + q
                for t in range(2):
                    parts[h, owner % 2, (owner // 2) % 4, owner // 8, 0, t] = grads[t][
                        q * R_DEV : (q + 1) * R_DEV
                    ].astype(BF16)

        def side_grads():
            leaf_rows = slice(LEAF_AT, Q_ROWS)
            grads = key_grads(slice(N_ROOT, N_ROOT + SPAN + L_DEV), leaf_rows)
            gain_part[0:8] += gain_term(grads[0], side[0, : SPAN + L_DEV, :])
            cols = pl.ds(pl.multiple_of(h * DH, DH), DH)
            rows = slice(R_DEV + B_DEV, ROWS)
            raw = k_ref[rows, cols].astype(F32)
            gk_ref[rows, cols] = norm_backward(
                raw, inverse_norm(raw), kgain_ref[...], grads[0][SPAN:]
            ).astype(BF16)
            gv_ref[rows, cols] = grads[1][SPAN:].astype(BF16)
            own_grads = key_grads(slice(N_ROOT, N_ROOT + SPAN), slice(GQ * R_DEV, LEAF_AT))
            gain_part[0:8] += gain_term(own_grads[0], side[0, SPAN + L_DEV :, :])
            for b in range(4):
                to_parent = jnp.where(parent == b, 1.0, 0.0)
                to_own = jnp.where(own_branch == b, 1.0, 0.0)
                for t in range(2):
                    both = grads[t][:SPAN] * to_parent + own_grads[t] * to_own
                    for q in range(4):
                        owner = 4 * b + q
                        parts[h, owner % 2, (owner // 2) % 4, owner // 8, 1, t] = both[
                            q * B_DEV : (q + 1) * B_DEV
                        ].astype(BF16)

        def query_grads(rb):
            rows = slice(rb * RB, (rb + 1) * RB)
            grads = dot(gscores[:N_ROOT, rows], kv[h, 0, 0], TN)
            if rb == 1:
                grads += dot(gscores[N_ROOT : N_ROOT + SPAN, rows], side[0, SPAN + L_DEV :, :], TN)
            if rb >= 2:
                grads += dot(gscores[N_ROOT:, rows], side[0, : SPAN + L_DEV, :], TN)
            grad_qn[rows, :] = grads * (inv_rows[rows, :] * SCALE)

        def finish_queries():
            for start, count, at in SEGMENTS:
                for g in range(GQ):
                    cols = pl.ds(pl.multiple_of(h * GQ * DH + g * DH, DH), DH)
                    rows = slice(start, start + count)
                    grads = grad_qn[at + g * count : at + (g + 1) * count, :]
                    raw = q_ref[rows, cols].astype(F32)
                    inverse = inverse_norm(raw)
                    gq_ref[rows, cols] = norm_backward(
                        raw, inverse, qgain_ref[...], grads
                    ).astype(BF16)
                    gain_part[8:16] += fold(grads * raw * inverse)

        scores_of(0)
        pl.when(h < HK - 1)(lambda: gather_b(h + 1))
        scores_of(1)
        scores_of(2)
        pl.when(h < HK - 1)(lambda: gather_c(h + 1))
        pl.when(h > 0)(lambda: reduce_a(h - 1))
        pl.when(h > 1)(lambda: reduce_c(h - 2))
        scores_of(3)
        scores_of(4)
        pl.when(h < HK - 1)(lambda: gather_d(h + 1))
        for n in range(4):
            root_grads(n)
        side_grads()
        r_core(h).start()
        pl.when(h > 0)(lambda: reduce_b(h - 1))
        for rb in range(5):
            query_grads(rb)
        finish_queries()
        pl.when(h < HK - 1)(lambda: gather_e(h + 1))
        pl.when(h > 1)(lambda: reduce_d(h - 2))
        return carry

    lax.fori_loop(0, HK, one_head, 0)

    def a_copy(step, target):
        return pltpu.make_async_remote_copy(
            src_ref=gain_seq.at[0],
            dst_ref=gain_seq.at[step],
            send_sem=a_send.at[step],
            recv_sem=a_recv.at[step],
            device_id=(me_leaf, target),
            device_id_type=MESH,
        )

    def b_copy(step, target):
        return pltpu.make_async_remote_copy(
            src_ref=gain_leaf.at[0],
            dst_ref=gain_leaf.at[step],
            send_sem=b_send.at[step],
            recv_sem=b_recv.at[step],
            device_id=(target, me),
            device_id_type=MESH,
        )

    def a_start(step, carry):
        a_copy(step, (me + step) % N_SEQ).start()
        return carry

    def b_start(step, carry):
        b_copy(step, (me_leaf + step) % n_leaf).start()
        return carry

    def a_wait(step, total):
        a_copy(step, (me + step) % N_SEQ).wait()
        return total + gain_seq[step]

    def b_wait(step, total):
        b_copy(step, (me_leaf + step) % n_leaf).wait()
        return total + gain_leaf[step]

    row = lax.broadcasted_iota(jnp.int32, (8, DH), 0)
    key_sum = jnp.sum(gain_part[0:8], axis=0, keepdims=True) / kgain_ref[...]
    query_sum = jnp.sum(gain_part[8:16], axis=0, keepdims=True)
    gain_seq[0] = jnp.where(row == 0, query_sum, key_sum)
    lax.fori_loop(1, N_SEQ, a_start, 0)
    reduce_a(HK - 1)
    reduce_c(HK - 2)
    gain_leaf[0] = lax.fori_loop(1, N_SEQ, a_wait, gain_seq[0])
    lax.fori_loop(1, n_leaf, b_start, 0)
    reduce_b(HK - 1)
    reduce_d(HK - 2)
    gains_ref[...] = lax.fori_loop(1, n_leaf, b_wait, gain_leaf[0])
    reduce_c(HK - 1)
    reduce_d(HK - 1)
    for h in range(HK):
        gather_sent(h)
        reduce_sent(h)


def on_device(
    query_raw, key_raw, value_raw, grad_out, query_gain, key_gain, leaf_parent, leaf_blocks
):
    n_leaf = lax.axis_size("leaf")
    vmem = pl.BlockSpec(memory_space=pltpu.VMEM)
    smem = pl.BlockSpec(memory_space=pltpu.SMEM)
    keys = N_ROOT + SPAN + L_DEV
    dma = pltpu.SemaphoreType.DMA
    grad_query, grad_key, grad_value, gains = pl.pallas_call(
        functools.partial(kernel, n_leaf),
        out_shape=(
            jax.ShapeDtypeStruct((ROWS, HQ * DH), BF16),
            jax.ShapeDtypeStruct((ROWS, HK * DH), BF16),
            jax.ShapeDtypeStruct((ROWS, HK * DH), BF16),
            jax.ShapeDtypeStruct((8, DH), F32),
        ),
        in_specs=[smem, smem] + [vmem] * 6,
        out_specs=(vmem,) * 4,
        scratch_shapes=[
            pltpu.VMEM((HK, 2, 2, N_ROOT, DH), BF16),
            pltpu.VMEM((HK, 2, L_DEV, DH), BF16),
            pltpu.VMEM((2, 2 * SPAN + L_DEV, DH), BF16),
            pltpu.VMEM((HK, Q_ROWS, DH), BF16),
            pltpu.VMEM((HK, Q_ROWS, DH), BF16),
            pltpu.VMEM((keys, Q_ROWS), BF16),
            pltpu.VMEM((keys, Q_ROWS), F32),
            pltpu.VMEM((keys, Q_ROWS), BF16),
            pltpu.VMEM((Q_ROWS, DH), BF16),
            pltpu.VMEM((Q_ROWS, DH), BF16),
            pltpu.VMEM((Q_ROWS, DH), F32),
            pltpu.VMEM((8, Q_ROWS), F32),
            pltpu.VMEM((Q_ROWS, DH), F32),
            pltpu.VMEM((HK, 2, 4, 2, 2, 2, R_DEV, DH), BF16),
            pltpu.VMEM((HK, 4, 2, 2, 2, R_DEV, DH), BF16),
            pltpu.VMEM((HK, 2, 2, 2, R_DEV, DH), BF16),
            pltpu.VMEM((HK, 2, 2, 2, 2, R_DEV, DH), BF16),
            pltpu.VMEM((HK, 2, 2, R_DEV, DH), BF16),
            pltpu.VMEM((HK, 2, 2, R_DEV, DH), F32),
            pltpu.VMEM((HK, 2, 2, R_DEV, DH), BF16),
            pltpu.VMEM((16, DH), F32),
            pltpu.VMEM((N_SEQ, 8, DH), F32),
            pltpu.VMEM((n_leaf, 8, DH), F32),
            dma((HK, N_G)),
            dma((HK, N_G)),
            dma((HK, N_R)),
            dma((HK, N_R)),
            dma((N_SEQ,)),
            dma((N_SEQ,)),
            dma((n_leaf,)),
            dma((n_leaf,)),
        ],
        compiler_params=pltpu.CompilerParams(
            collective_id=0, has_side_effects=True, vmem_limit_bytes=60 * 2**20
        ),
        name="attention_backward",
    )(
        leaf_parent,
        leaf_blocks,
        query_raw[0],
        key_raw[0],
        value_raw[0],
        grad_out[0],
        query_gain.reshape(1, DH),
        key_gain.reshape(1, DH),
    )
    return grad_query[None], grad_key[None], grad_value[None], gains[0], gains[1]


def solution(mesh):
    return jax.shard_map(
        on_device,
        mesh=mesh,
        in_specs=(
            P("leaf", "seq", None),
            P("leaf", "seq", None),
            P("leaf", "seq", None),
            P("leaf", "seq", None),
            P(),
            P(),
            P("leaf", "seq"),
            P("leaf", "seq"),
        ),
        out_specs=(
            P("leaf", "seq", None),
            P("leaf", "seq", None),
            P("leaf", "seq", None),
            P(),
            P(),
        ),
        check_vma=False,
    )
```

```python
import functools
import math

import jax
import jax.numpy as jnp
from jax import lax
from jax.experimental import pallas as pl
from jax.experimental.pallas import tpu as pltpu
from jax.sharding import PartitionSpec as P

HQ = 16
HK = 4
DH = 128
GQ = HQ // HK
R_DEV = 64
B_DEV = 64
LEAF_BLOCK = 64
L_DEV = 192
ROWS = 320
N_SEQ = 16
N_ROOT = R_DEV * N_SEQ
SPAN = 256
RB = 256
Q_ROWS = ROWS * GQ
LEAF_AT = GQ * (R_DEV + B_DEV)
EPS = 1e-06
SCALE = 1.0 / math.sqrt(DH)
EXP2_SCALE = SCALE / math.log(2.0)

F32 = jnp.float32
BF16 = jnp.bfloat16
MESH = pl.DeviceIdType.MESH
NT = (((1,), (1,)), ((), ()))
NN = (((1,), (0,)), ((), ()))
TN = (((0,), (0,)), ((), ()))

SEGMENTS = ((0, R_DEV, 0), (R_DEV, B_DEV, GQ * R_DEV), (R_DEV + B_DEV, L_DEV, LEAF_AT))

CHIPS = 8
HALVES = 2 * HK


def dot(left, right, dims):
    return lax.dot_general(left, right, dims, preferred_element_type=F32)


def inverse_norm(values):
    return lax.rsqrt(jnp.mean(values * values, axis=-1, keepdims=True) + EPS)


def norm_backward(values, inverse, gain, upstream):
    scaled = upstream * gain
    mean = jnp.mean(scaled * values, axis=-1, keepdims=True)
    return inverse * scaled - values * (inverse * inverse * inverse * mean)


def fold(array):
    return jnp.sum(array.reshape(array.shape[0] // 8, 8, array.shape[1]), axis=0)


def kernel(
    n_leaf,
    parent_ref,
    blocks_ref,
    q_hbm,
    k_ref,
    v_ref,
    u_hbm,
    qgain_ref,
    kgain_ref,
    gq_hbm,
    gk_ref,
    gv_ref,
    gains_ref,
    q_ref,
    u_ref,
    gq_ref,
    kv,
    leaf_kv,
    side,
    qn,
    up,
    expo,
    gprobs,
    gscores,
    q_scaled,
    up_scaled,
    inv_rows,
    dot_rows,
    sums,
    grad_qn,
    parts,
    from_core,
    from_chip,
    gain_part,
    gain_seq,
    gain_leaf,
    g_send,
    g_recv,
    r_send,
    r_recv,
    a_send,
    a_recv,
    b_send,
    b_recv,
    io_sem,
):
    me = lax.axis_index("seq")
    me_leaf = lax.axis_index("leaf")
    x = me // 8
    y = (me // 2) % 4
    c = me % 2
    def place(px, py, pc):
        return px * 8 + py * 2 + pc

    dev_core = place(x, y, 1 - c)
    parent = parent_ref[0, 0]
    leaf_length = blocks_ref[0, 0] * LEAF_BLOCK
    own_branch = me // 4

    load_q = pltpu.make_async_copy(q_hbm, q_ref, io_sem.at[HK])
    load_u = pltpu.make_async_copy(u_hbm, u_ref, io_sem.at[HK + 1])

    barrier = pltpu.get_barrier_semaphore()

    def greet_seq(step, carry):
        pl.semaphore_signal(
            barrier, inc=1, device_id=(me_leaf, (me + step) % N_SEQ), device_id_type=MESH
        )
        return carry

    def greet_leaf(step, carry):
        pl.semaphore_signal(
            barrier, inc=1, device_id=((me_leaf + step) % n_leaf, me), device_id_type=MESH
        )
        return carry

    lax.fori_loop(1, N_SEQ, greet_seq, 0)
    lax.fori_loop(1, n_leaf, greet_leaf, 0)

    load_q.start()
    load_u.start()


    def prepare_keys(h):
        cols = slice(h * DH, (h + 1) * DH)
        raw = k_ref[:, cols].astype(F32)
        normed = (raw * inverse_norm(raw) * kgain_ref[...]).astype(BF16)
        values = v_ref[:, cols]
        kv[h, 0, 0, x, y, c] = normed[:R_DEV]
        kv[h, 1, 0, x, y, c] = normed[R_DEV : R_DEV + B_DEV]
        leaf_kv[h, 0] = normed[R_DEV + B_DEV :]
        kv[h, 0, 1, x, y, c] = values[:R_DEV]
        kv[h, 1, 1, x, y, c] = values[R_DEV : R_DEV + B_DEV]
        leaf_kv[h, 1] = values[R_DEV + B_DEV :]

    prepare_keys(0)
    pl.semaphore_wait(barrier, N_SEQ - 1 + n_leaf - 1)

    def chip_at(number, sign):
        other = number // 4
        return x + other * (1 - 2 * x), (y + sign * (number % 4)) % 4

    def g_copy(half, number, px, py, target):
        ref = kv.at[half // 2, half % 2, :, px, py, c]
        return pltpu.make_async_remote_copy(
            src_ref=ref,
            dst_ref=ref,
            send_sem=g_send.at[half, number],
            recv_sem=g_recv.at[half, number],
            device_id=(me_leaf, target),
            device_id_type=MESH,
        )

    def g_core(half, core):
        ref = kv.at[half // 2, half % 2, :, :, :, core]
        return pltpu.make_async_remote_copy(
            src_ref=ref,
            dst_ref=ref,
            send_sem=g_send.at[half, 0],
            recv_sem=g_recv.at[half, 0],
            device_id=(me_leaf, dev_core),
            device_id_type=MESH,
        )

    def gather_a(half):
        for number in range(1, CHIPS):
            px, py = chip_at(number, 1)
            g_copy(half, number, x, y, place(px, py, c)).start()

    def gather_b(half):
        for number in range(1, CHIPS):
            px, py = chip_at(number, 3)
            g_copy(half, number, px, py, place(px, py, c)).wait_recv()
        g_core(half, c).start()

    def gather_c(half):
        g_core(half, 1 - c).wait_recv()

    def gather_sent(half):
        for number in range(1, CHIPS):
            px, py = chip_at(number, 1)
            g_copy(half, number, x, y, place(px, py, c)).wait_send()
        g_core(half, c).wait_send()

    def r_core(half):
        return pltpu.make_async_remote_copy(
            src_ref=parts.at[half, 1 - c],
            dst_ref=from_core.at[half],
            send_sem=r_send.at[half, 0],
            recv_sem=r_recv.at[half, 0],
            device_id=(me_leaf, dev_core),
            device_id_type=MESH,
        )

    def r_copy(half, number):
        px, py = chip_at(number, 1)
        return pltpu.make_async_remote_copy(
            src_ref=parts.at[half, c, px, py],
            dst_ref=from_chip.at[half, number],
            send_sem=r_send.at[half, number],
            recv_sem=r_recv.at[half, number],
            device_id=(me_leaf, place(px, py, c)),
            device_id_type=MESH,
        )

    def reduce_a(half):
        r_core(half).wait_recv()
        for px in range(2):
            for py in range(4):
                parts[half, c, px, py] = (
                    parts[half, c, px, py].astype(F32) + from_core[half, px, py].astype(F32)
                ).astype(BF16)
        for number in range(1, CHIPS):
            r_copy(half, number).start()

    def reduce_b(half):
        for number in range(1, CHIPS):
            r_copy(half, number).wait_recv()
        total = parts[half, c, x, y].astype(F32)
        for number in range(1, CHIPS):
            total += from_chip[half, number].astype(F32)
        cols = pl.ds(pl.multiple_of((half // 2) * DH, DH), DH)
        rows = pl.ds(pl.multiple_of((half % 2) * R_DEV, R_DEV), R_DEV)
        raw = k_ref[rows, cols].astype(F32)
        gk_ref[rows, cols] = norm_backward(
            raw, inverse_norm(raw), kgain_ref[...], total[0]
        ).astype(BF16)
        gv_ref[rows, cols] = total[1].astype(BF16)

    def reduce_sent(half):
        r_core(half).wait_send()
        for number in range(1, CHIPS):
            r_copy(half, number).wait_send()

    def prepare(h):
        for start, count, at in SEGMENTS:
            for g in range(GQ):
                cols = pl.ds(pl.multiple_of(h * GQ * DH + g * DH, DH), DH)
                rows = slice(start, start + count)
                dst = slice(at + g * count, at + (g + 1) * count)
                raw = q_ref[rows, cols].astype(F32)
                qn[h, dst, :] = (raw * inverse_norm(raw) * qgain_ref[...]).astype(BF16)
                grads = u_ref[rows, cols]
                if start == R_DEV + B_DEV:
                    ids = lax.broadcasted_iota(jnp.int32, (count, DH), 0)
                    grads = jnp.where(ids < leaf_length, grads.astype(F32), 0.0).astype(BF16)
                up[h, dst, :] = grads

    for half in range(2):
        gather_a(half)
    for h in range(1, HK):
        prepare_keys(h)
    for half in range(2, HALVES):
        gather_a(half)
    load_q.wait()
    load_u.wait()
    for h in range(HK):
        prepare(h)
    gather_b(0)
    gather_b(1)
    gather_c(0)
    gain_part[...] = jnp.zeros_like(gain_part)

    def one_head(h, carry):
        def pick_side():
            for t in range(2):
                picked = kv[h, 1, t, 0, 0:2].reshape(SPAN, DH)
                for b in range(1, 4):
                    picked = lax.select_n(
                        parent == b,
                        picked,
                        kv[h, 1, t, b // 2, b % 2 * 2 : b % 2 * 2 + 2].reshape(SPAN, DH),
                    )
                side[h, t, 0:SPAN, :] = picked
                side[h, t, SPAN : SPAN + L_DEV, :] = leaf_kv[h, t]
                side[h, t, SPAN + L_DEV :, :] = kv[h, 1, t, x, pl.ds(y // 2 * 2, 2)].reshape(
                    SPAN, DH
                )

        def key_ids(count):
            return lax.broadcasted_iota(jnp.int32, (count, RB), 0)

        def row_ids(count, first, period):
            return (lax.broadcasted_iota(jnp.int32, (count, RB), 1) + first) % period

        def chunk(rb, keys, values, dst, allowed):
            rows = slice(rb * RB, (rb + 1) * RB)
            count = keys.shape[0]
            e = jnp.exp2(dot(keys, qn[h, rows, :], NT) * EXP2_SCALE)
            if allowed is not None:
                e = jnp.where(allowed, e, 0.0)
            gp = dot(values, up[h, rows, :], NT)
            expo[dst : dst + count, rows] = e.astype(BF16)
            gprobs[dst : dst + count, rows] = gp
            return fold(e), fold(e * gp)

        def root_block(t, n):
            return kv[h, 0, t, n // 2, n % 2 * 2 : n % 2 * 2 + 2].reshape(SPAN, DH)

        def root_scores(rb):
            found = []
            for n in range(N_ROOT // SPAN):
                allowed = None
                if rb == 0:
                    allowed = key_ids(SPAN) + n * SPAN <= row_ids(SPAN, 0, R_DEV) + me * R_DEV
                found.append(chunk(rb, root_block(0, n), root_block(1, n), n * SPAN, allowed))
            rows = slice(rb * RB, (rb + 1) * RB)
            sums[0, :, rows] = sum(f[0] for f in found)
            sums[1, :, rows] = sum(f[1] for f in found)

        def side_scores(rb):
            rows = slice(rb * RB, (rb + 1) * RB)
            found = [(sums[0, :, rows], sums[1, :, rows])]
            if rb == 1:
                allowed = key_ids(SPAN) <= row_ids(SPAN, 0, B_DEV) + (me % 4) * B_DEV
                keys = slice(SPAN + L_DEV, 2 * SPAN + L_DEV)
                found.append(chunk(rb, side[h, 0, keys, :], side[h, 1, keys, :], N_ROOT, allowed))
            if rb >= 2:
                found.append(
                    chunk(rb, side[h, 0, :SPAN, :], side[h, 1, :SPAN, :], N_ROOT, None)
                )
                ids = key_ids(L_DEV)
                allowed = (ids <= row_ids(L_DEV, (rb - 2) * RB, L_DEV)) & (ids < leaf_length)
                keys = slice(SPAN, SPAN + L_DEV)
                found.append(
                    chunk(rb, side[h, 0, keys, :], side[h, 1, keys, :], N_ROOT + SPAN, allowed)
                )
            total = jnp.sum(sum(f[0] for f in found), axis=0, keepdims=True)
            weighted = jnp.sum(sum(f[1] for f in found), axis=0, keepdims=True)
            inverse = 1.0 / total
            dot_rows[:, rows] = jnp.broadcast_to(weighted * inverse, (8, RB))
            spread = jnp.transpose(jnp.broadcast_to(inverse, (DH, RB)))
            inv_rows[h, rows, :] = spread
            q_scaled[rows, :] = (qn[h, rows, :].astype(F32) * (spread * SCALE)).astype(BF16)
            up_scaled[rows, :] = (up[h, rows, :].astype(F32) * spread).astype(BF16)

        def key_grads(keys, rows):
            gs = (
                expo[keys, rows].astype(F32) * (gprobs[keys, rows] - dot_rows[0:1, rows])
            ).astype(BF16)
            gscores[h, keys, rows] = gs
            return (
                dot(gs, q_scaled[rows, :], NN),
                dot(expo[keys, rows], up_scaled[rows, :], NN),
            )

        def gain_term(grad_kn, keys):
            return fold(grad_kn * keys.astype(F32))

        def root_grads(n):
            keys = slice(n * SPAN, (n + 1) * SPAN)
            grads = key_grads(keys, slice(0, Q_ROWS))
            gain_part[0:8] += gain_term(grads[0], root_block(0, n))
            for q in range(4):
                owner = 4 * n + q
                for t in range(2):
                    parts[2 * h, owner % 2, owner // 8, (owner // 2) % 4, t] = grads[t][
                        q * R_DEV : (q + 1) * R_DEV
                    ].astype(BF16)

        def side_grads():
            leaf_rows = slice(LEAF_AT, Q_ROWS)
            grads = key_grads(slice(N_ROOT, N_ROOT + SPAN + L_DEV), leaf_rows)
            gain_part[0:8] += gain_term(grads[0], side[h, 0, : SPAN + L_DEV, :])
            cols = pl.ds(pl.multiple_of(h * DH, DH), DH)
            rows = slice(R_DEV + B_DEV, ROWS)
            raw = k_ref[rows, cols].astype(F32)
            gk_ref[rows, cols] = norm_backward(
                raw, inverse_norm(raw), kgain_ref[...], grads[0][SPAN:]
            ).astype(BF16)
            gv_ref[rows, cols] = grads[1][SPAN:].astype(BF16)
            own_grads = key_grads(slice(N_ROOT, N_ROOT + SPAN), slice(GQ * R_DEV, LEAF_AT))
            gain_part[0:8] += gain_term(own_grads[0], side[h, 0, SPAN + L_DEV :, :])
            for b in range(4):
                to_parent = jnp.where(parent == b, 1.0, 0.0)
                to_own = jnp.where(own_branch == b, 1.0, 0.0)
                for t in range(2):
                    both = grads[t][:SPAN] * to_parent + own_grads[t] * to_own
                    for q in range(4):
                        owner = 4 * b + q
                        parts[2 * h + 1, owner % 2, owner // 8, (owner // 2) % 4, t] = both[
                            q * B_DEV : (q + 1) * B_DEV
                        ].astype(BF16)

        for rb in range(5):
            root_scores(rb)

        @pl.when(h < HK - 1)
        def _():
            gather_b(2 * h + 2)
            gather_b(2 * h + 3)

        @pl.when(h > 0)
        def _():
            reduce_a(2 * h - 2)
            reduce_a(2 * h - 1)

        @pl.when(h > 1)
        def _():
            reduce_b(2 * h - 4)
            reduce_b(2 * h - 3)

        gather_c(2 * h + 1)
        pick_side()
        for rb in range(5):
            side_scores(rb)
        for n in range(4):
            root_grads(n)
        r_core(2 * h).start()
        side_grads()
        r_core(2 * h + 1).start()

        @pl.when(h < HK - 1)
        def _():
            gather_c(2 * h + 2)

        return carry

    lax.fori_loop(0, HK, one_head, 0)

    def store_q(h):
        cols = pl.ds(h * GQ * DH, GQ * DH)
        return pltpu.make_async_copy(gq_ref.at[:, cols], gq_hbm.at[:, cols], io_sem.at[h])

    def queries_of(h):
        def query_grads(rb):
            rows = slice(rb * RB, (rb + 1) * RB)
            grads = dot(gscores[h, :N_ROOT, rows], kv[h, 0, 0].reshape(N_ROOT, DH), TN)
            if rb == 1:
                grads += dot(gscores[h, N_ROOT : N_ROOT + SPAN, rows], side[h, 0, SPAN + L_DEV :, :], TN)
            if rb >= 2:
                grads += dot(gscores[h, N_ROOT:, rows], side[h, 0, : SPAN + L_DEV, :], TN)
            grad_qn[rows, :] = grads * (inv_rows[h, rows, :] * SCALE)

        def finish_queries():
            for start, count, at in SEGMENTS:
                for g in range(GQ):
                    cols = pl.ds(pl.multiple_of(h * GQ * DH + g * DH, DH), DH)
                    rows = slice(start, start + count)
                    grads = grad_qn[at + g * count : at + (g + 1) * count, :]
                    raw = q_ref[rows, cols].astype(F32)
                    inverse = inverse_norm(raw)
                    gq_ref[rows, cols] = norm_backward(
                        raw, inverse, qgain_ref[...], grads
                    ).astype(BF16)
                    gain_part[8:16] += fold(grads * raw * inverse)

        for rb in range(5):
            query_grads(rb)
        finish_queries()
        store_q(h).start()

    def a_copy(step, target):
        return pltpu.make_async_remote_copy(
            src_ref=gain_seq.at[0],
            dst_ref=gain_seq.at[step],
            send_sem=a_send.at[step],
            recv_sem=a_recv.at[step],
            device_id=(me_leaf, target),
            device_id_type=MESH,
        )

    def b_copy(step, target):
        return pltpu.make_async_remote_copy(
            src_ref=gain_leaf.at[0],
            dst_ref=gain_leaf.at[step],
            send_sem=b_send.at[step],
            recv_sem=b_recv.at[step],
            device_id=(target, me),
            device_id_type=MESH,
        )

    def a_start(step, carry):
        a_copy(step, (me + step) % N_SEQ).start()
        return carry

    def b_start(step, carry):
        b_copy(step, (me_leaf + step) % n_leaf).start()
        return carry

    def a_wait(step, total):
        a_copy(step, (me + step) % N_SEQ).wait()
        return total + gain_seq[step]

    def b_wait(step, total):
        b_copy(step, (me_leaf + step) % n_leaf).wait()
        return total + gain_leaf[step]

    root, branch = HALVES - 2, HALVES - 1
    reduce_a(root)
    queries_of(0)
    reduce_a(branch)
    queries_of(1)
    queries_of(2)
    reduce_b(root - 2)
    reduce_b(branch - 2)
    queries_of(3)
    row = lax.broadcasted_iota(jnp.int32, (8, DH), 0)
    key_sum = jnp.sum(gain_part[0:8], axis=0, keepdims=True) / kgain_ref[...]
    query_sum = jnp.sum(gain_part[8:16], axis=0, keepdims=True)
    gain_seq[0] = jnp.where(row == 0, query_sum, key_sum)
    lax.fori_loop(1, N_SEQ, a_start, 0)
    reduce_b(root)
    gain_leaf[0] = lax.fori_loop(1, N_SEQ, a_wait, gain_seq[0])
    lax.fori_loop(1, n_leaf, b_start, 0)
    reduce_b(branch)
    gains_ref[...] = lax.fori_loop(1, n_leaf, b_wait, gain_leaf[0])
    for half in range(HALVES):
        gather_sent(half)
        reduce_sent(half)
    for h in range(HK):
        store_q(h).wait()


def on_device(
    query_raw, key_raw, value_raw, grad_out, query_gain, key_gain, leaf_parent, leaf_blocks
):
    n_leaf = lax.axis_size("leaf")
    vmem = pl.BlockSpec(memory_space=pltpu.VMEM)
    smem = pl.BlockSpec(memory_space=pltpu.SMEM)
    hbm = pl.BlockSpec(memory_space=pl.ANY)
    keys = N_ROOT + SPAN + L_DEV
    dma = pltpu.SemaphoreType.DMA
    grad_query, grad_key, grad_value, gains = pl.pallas_call(
        functools.partial(kernel, n_leaf),
        out_shape=(
            jax.ShapeDtypeStruct((ROWS, HQ * DH), BF16),
            jax.ShapeDtypeStruct((ROWS, HK * DH), BF16),
            jax.ShapeDtypeStruct((ROWS, HK * DH), BF16),
            jax.ShapeDtypeStruct((8, DH), F32),
        ),
        in_specs=[smem, smem, hbm, vmem, vmem, hbm, vmem, vmem],
        out_specs=(hbm, vmem, vmem, vmem),
        scratch_shapes=[
            pltpu.VMEM((ROWS, HQ * DH), BF16),
            pltpu.VMEM((ROWS, HQ * DH), BF16),
            pltpu.VMEM((ROWS, HQ * DH), BF16),
            pltpu.VMEM((HK, 2, 2, 2, 4, 2, R_DEV, DH), BF16),
            pltpu.VMEM((HK, 2, L_DEV, DH), BF16),
            pltpu.VMEM((HK, 2, 2 * SPAN + L_DEV, DH), BF16),
            pltpu.VMEM((HK, Q_ROWS, DH), BF16),
            pltpu.VMEM((HK, Q_ROWS, DH), BF16),
            pltpu.VMEM((keys, Q_ROWS), BF16),
            pltpu.VMEM((keys, Q_ROWS), F32),
            pltpu.VMEM((HK, keys, Q_ROWS), BF16),
            pltpu.VMEM((Q_ROWS, DH), BF16),
            pltpu.VMEM((Q_ROWS, DH), BF16),
            pltpu.VMEM((HK, Q_ROWS, DH), F32),
            pltpu.VMEM((8, Q_ROWS), F32),
            pltpu.VMEM((2, 8, Q_ROWS), F32),
            pltpu.VMEM((Q_ROWS, DH), F32),
            pltpu.VMEM((HALVES, 2, 2, 4, 2, R_DEV, DH), BF16),
            pltpu.VMEM((HALVES, 2, 4, 2, R_DEV, DH), BF16),
            pltpu.VMEM((HALVES, CHIPS, 2, R_DEV, DH), BF16),
            pltpu.VMEM((16, DH), F32),
            pltpu.VMEM((N_SEQ, 8, DH), F32),
            pltpu.VMEM((n_leaf, 8, DH), F32),
            dma((HALVES, CHIPS)),
            dma((HALVES, CHIPS)),
            dma((HALVES, CHIPS)),
            dma((HALVES, CHIPS)),
            dma((N_SEQ,)),
            dma((N_SEQ,)),
            dma((n_leaf,)),
            dma((n_leaf,)),
            dma((HK + 2,)),
        ],
        compiler_params=pltpu.CompilerParams(
            collective_id=0, has_side_effects=True, vmem_limit_bytes=60 * 2**20
        ),
        name="attention_backward",
    )(
        leaf_parent,
        leaf_blocks,
        query_raw[0],
        key_raw[0],
        value_raw[0],
        grad_out[0],
        query_gain.reshape(1, DH),
        key_gain.reshape(1, DH),
    )
    return grad_query[None], grad_key[None], grad_value[None], gains[0], gains[1]


def solution(mesh):
    return jax.shard_map(
        on_device,
        mesh=mesh,
        in_specs=(
            P("leaf", "seq", None),
            P("leaf", "seq", None),
            P("leaf", "seq", None),
            P("leaf", "seq", None),
            P(),
            P(),
            P("leaf", "seq"),
            P("leaf", "seq"),
        ),
        out_specs=(
            P("leaf", "seq", None),
            P("leaf", "seq", None),
            P("leaf", "seq", None),
            P(),
            P(),
        ),
        check_vma=False,
    )
```

```python
import functools
import math

import jax
import jax.numpy as jnp
from jax import lax
from jax.experimental import pallas as pl
from jax.experimental.pallas import tpu as pltpu
from jax.sharding import PartitionSpec as P

HQ = 16
HK = 4
DH = 128
GQ = HQ // HK
R_DEV = 64
B_DEV = 64
LEAF_BLOCK = 64
L_DEV = 192
ROWS = 320
N_SEQ = 16
N_ROOT = R_DEV * N_SEQ
SPAN = 256
RB = 256
Q_ROWS = ROWS * GQ
LEAF_AT = GQ * (R_DEV + B_DEV)
EPS = 1e-06
SCALE = 1.0 / math.sqrt(DH)
EXP2_SCALE = SCALE / math.log(2.0)

F32 = jnp.float32
BF16 = jnp.bfloat16
MESH = pl.DeviceIdType.MESH
NT = (((1,), (1,)), ((), ()))
NN = (((1,), (0,)), ((), ()))
TN = (((0,), (0,)), ((), ()))

SEGMENTS = ((0, R_DEV, 0), (R_DEV, B_DEV, GQ * R_DEV), (R_DEV + B_DEV, L_DEV, LEAF_AT))

CHIPS = 8
HALVES = 2 * HK


def dot(left, right, dims):
    return lax.dot_general(left, right, dims, preferred_element_type=F32)


def inverse_norm(values):
    return lax.rsqrt(jnp.mean(values * values, axis=-1, keepdims=True) + EPS)


def norm_backward(values, inverse, gain, upstream):
    scaled = upstream * gain
    mean = jnp.mean(scaled * values, axis=-1, keepdims=True)
    return inverse * scaled - values * (inverse * inverse * inverse * mean)


def fold(array):
    return jnp.sum(array.reshape(array.shape[0] // 8, 8, array.shape[1]), axis=0)


def kernel(
    n_leaf,
    parent_ref,
    blocks_ref,
    q_hbm,
    k_ref,
    v_ref,
    u_hbm,
    qgain_ref,
    kgain_ref,
    gq_hbm,
    gk_ref,
    gv_ref,
    gains_ref,
    q_ref,
    u_ref,
    gq_ref,
    kv,
    leaf_kv,
    side,
    qn,
    up,
    expo,
    gprobs,
    gscores,
    q_scaled,
    up_scaled,
    inv_rows,
    dot_rows,
    sums,
    grad_qn,
    parts,
    from_core,
    from_chip,
    gain_part,
    gain_seq,
    gain_leaf,
    g_send,
    g_recv,
    r_send,
    r_recv,
    a_send,
    a_recv,
    b_send,
    b_recv,
    io_sem,
):
    me = lax.axis_index("seq")
    me_leaf = lax.axis_index("leaf")
    x = me // 8
    y = (me // 2) % 4
    c = me % 2
    def place(px, py, pc):
        return px * 8 + py * 2 + pc

    dev_core = place(x, y, 1 - c)
    parent = parent_ref[0, 0]
    leaf_length = blocks_ref[0, 0] * LEAF_BLOCK
    own_branch = me // 4

    load_q = pltpu.make_async_copy(q_hbm, q_ref, io_sem.at[HK])
    load_u = pltpu.make_async_copy(u_hbm, u_ref, io_sem.at[HK + 1])

    barrier = pltpu.get_barrier_semaphore()

    def greet_seq(step, carry):
        pl.semaphore_signal(
            barrier, inc=1, device_id=(me_leaf, (me + step) % N_SEQ), device_id_type=MESH
        )
        return carry

    def greet_leaf(step, carry):
        pl.semaphore_signal(
            barrier, inc=1, device_id=((me_leaf + step) % n_leaf, me), device_id_type=MESH
        )
        return carry

    lax.fori_loop(1, N_SEQ, greet_seq, 0)
    lax.fori_loop(1, n_leaf, greet_leaf, 0)

    load_q.start()
    load_u.start()


    def prepare_keys(h):
        cols = slice(h * DH, (h + 1) * DH)
        raw = k_ref[:, cols].astype(F32)
        normed = (raw * inverse_norm(raw) * kgain_ref[...]).astype(BF16)
        values = v_ref[:, cols]
        kv[h, 0, 0, x, y, c] = normed[:R_DEV]
        kv[h, 1, 0, x, y, c] = normed[R_DEV : R_DEV + B_DEV]
        leaf_kv[h, 0] = normed[R_DEV + B_DEV :]
        kv[h, 0, 1, x, y, c] = values[:R_DEV]
        kv[h, 1, 1, x, y, c] = values[R_DEV : R_DEV + B_DEV]
        leaf_kv[h, 1] = values[R_DEV + B_DEV :]

    prepare_keys(0)
    pl.semaphore_wait(barrier, N_SEQ - 1 + n_leaf - 1)

    def chip_at(number, sign):
        other = number // 4
        return x + other * (1 - 2 * x), (y + sign * (number % 4)) % 4

    def g_copy(half, number, px, py, target):
        ref = kv.at[half // 2, half % 2, :, px, py, c]
        return pltpu.make_async_remote_copy(
            src_ref=ref,
            dst_ref=ref,
            send_sem=g_send.at[half, number],
            recv_sem=g_recv.at[half, number],
            device_id=(me_leaf, target),
            device_id_type=MESH,
        )

    def g_core(half, core):
        ref = kv.at[half // 2, half % 2, :, :, :, core]
        return pltpu.make_async_remote_copy(
            src_ref=ref,
            dst_ref=ref,
            send_sem=g_send.at[half, 0],
            recv_sem=g_recv.at[half, 0],
            device_id=(me_leaf, dev_core),
            device_id_type=MESH,
        )

    def gather_a(half):
        for number in range(1, CHIPS):
            px, py = chip_at(number, 1)
            g_copy(half, number, x, y, place(px, py, c)).start()

    def gather_b(half):
        for number in range(1, CHIPS):
            px, py = chip_at(number, 3)
            g_copy(half, number, px, py, place(px, py, c)).wait_recv()
        g_core(half, c).start()

    def gather_c(half):
        g_core(half, 1 - c).wait_recv()

    def gather_sent(half):
        for number in range(1, CHIPS):
            px, py = chip_at(number, 1)
            g_copy(half, number, x, y, place(px, py, c)).wait_send()
        g_core(half, c).wait_send()

    def r_core(half):
        return pltpu.make_async_remote_copy(
            src_ref=parts.at[half, 1 - c],
            dst_ref=from_core.at[half],
            send_sem=r_send.at[half, 0],
            recv_sem=r_recv.at[half, 0],
            device_id=(me_leaf, dev_core),
            device_id_type=MESH,
        )

    def r_copy(half, number):
        px, py = chip_at(number, 1)
        return pltpu.make_async_remote_copy(
            src_ref=parts.at[half, c, px, py],
            dst_ref=from_chip.at[half, number],
            send_sem=r_send.at[half, number],
            recv_sem=r_recv.at[half, number],
            device_id=(me_leaf, place(px, py, c)),
            device_id_type=MESH,
        )

    def reduce_a(half):
        r_core(half).wait_recv()
        for px in range(2):
            for py in range(4):
                parts[half, c, px, py] = (
                    parts[half, c, px, py].astype(F32) + from_core[half, px, py].astype(F32)
                ).astype(BF16)
        for number in range(1, CHIPS):
            r_copy(half, number).start()

    def reduce_b(half):
        for number in range(1, CHIPS):
            r_copy(half, number).wait_recv()
        total = parts[half, c, x, y].astype(F32)
        for number in range(1, CHIPS):
            total += from_chip[half, number].astype(F32)
        cols = pl.ds(pl.multiple_of((half // 2) * DH, DH), DH)
        rows = pl.ds(pl.multiple_of((half % 2) * R_DEV, R_DEV), R_DEV)
        raw = k_ref[rows, cols].astype(F32)
        gk_ref[rows, cols] = norm_backward(
            raw, inverse_norm(raw), kgain_ref[...], total[0]
        ).astype(BF16)
        gv_ref[rows, cols] = total[1].astype(BF16)

    def reduce_sent(half):
        r_core(half).wait_send()
        for number in range(1, CHIPS):
            r_copy(half, number).wait_send()

    def prepare(h):
        for start, count, at in SEGMENTS:
            for g in range(GQ):
                cols = pl.ds(pl.multiple_of(h * GQ * DH + g * DH, DH), DH)
                rows = slice(start, start + count)
                dst = slice(at + g * count, at + (g + 1) * count)
                raw = q_ref[rows, cols].astype(F32)
                qn[h, dst, :] = (raw * inverse_norm(raw) * qgain_ref[...]).astype(BF16)
                grads = u_ref[rows, cols]
                if start == R_DEV + B_DEV:
                    ids = lax.broadcasted_iota(jnp.int32, (count, DH), 0)
                    grads = jnp.where(ids < leaf_length, grads.astype(F32), 0.0).astype(BF16)
                up[h, dst, :] = grads

    for half in range(2):
        gather_a(half)
    for h in range(1, HK):
        prepare_keys(h)
    for half in range(2, HALVES):
        gather_a(half)
    load_q.wait()
    load_u.wait()
    for h in range(HK):
        prepare(h)
    gather_b(0)
    gather_c(0)
    gain_part[...] = jnp.zeros_like(gain_part)

    def one_head(h, carry):
        def pick_side():
            for t in range(2):
                picked = kv[h, 1, t, 0, 0:2].reshape(SPAN, DH)
                for b in range(1, 4):
                    picked = lax.select_n(
                        parent == b,
                        picked,
                        kv[h, 1, t, b // 2, b % 2 * 2 : b % 2 * 2 + 2].reshape(SPAN, DH),
                    )
                side[h, t, 0:SPAN, :] = picked
                side[h, t, SPAN : SPAN + L_DEV, :] = leaf_kv[h, t]
                side[h, t, SPAN + L_DEV :, :] = kv[h, 1, t, x, pl.ds(y // 2 * 2, 2)].reshape(
                    SPAN, DH
                )

        def key_ids(count):
            return lax.broadcasted_iota(jnp.int32, (count, RB), 0)

        def row_ids(count, first, period):
            return (lax.broadcasted_iota(jnp.int32, (count, RB), 1) + first) % period

        def chunk(rb, keys, values, dst, allowed):
            rows = slice(rb * RB, (rb + 1) * RB)
            count = keys.shape[0]
            e = jnp.exp2(dot(keys, qn[h, rows, :], NT) * EXP2_SCALE)
            if allowed is not None:
                e = jnp.where(allowed, e, 0.0)
            gp = dot(values, up[h, rows, :], NT)
            expo[dst : dst + count, rows] = e.astype(BF16)
            gprobs[dst : dst + count, rows] = gp
            return fold(e), fold(e * gp)

        def root_block(t, n):
            return kv[h, 0, t, n // 2, n % 2 * 2 : n % 2 * 2 + 2].reshape(SPAN, DH)

        def root_scores(rb):
            found = []
            for n in range(N_ROOT // SPAN):
                allowed = None
                if rb == 0:
                    allowed = key_ids(SPAN) + n * SPAN <= row_ids(SPAN, 0, R_DEV) + me * R_DEV
                found.append(chunk(rb, root_block(0, n), root_block(1, n), n * SPAN, allowed))
            rows = slice(rb * RB, (rb + 1) * RB)
            sums[0, :, rows] = sum(f[0] for f in found)
            sums[1, :, rows] = sum(f[1] for f in found)

        def side_scores(rb):
            rows = slice(rb * RB, (rb + 1) * RB)
            found = [(sums[0, :, rows], sums[1, :, rows])]
            if rb == 1:
                allowed = key_ids(SPAN) <= row_ids(SPAN, 0, B_DEV) + (me % 4) * B_DEV
                keys = slice(SPAN + L_DEV, 2 * SPAN + L_DEV)
                found.append(chunk(rb, side[h, 0, keys, :], side[h, 1, keys, :], N_ROOT, allowed))
            if rb >= 2:
                found.append(
                    chunk(rb, side[h, 0, :SPAN, :], side[h, 1, :SPAN, :], N_ROOT, None)
                )
                ids = key_ids(L_DEV)
                allowed = (ids <= row_ids(L_DEV, (rb - 2) * RB, L_DEV)) & (ids < leaf_length)
                keys = slice(SPAN, SPAN + L_DEV)
                found.append(
                    chunk(rb, side[h, 0, keys, :], side[h, 1, keys, :], N_ROOT + SPAN, allowed)
                )
            total = jnp.sum(sum(f[0] for f in found), axis=0, keepdims=True)
            weighted = jnp.sum(sum(f[1] for f in found), axis=0, keepdims=True)
            inverse = 1.0 / total
            dot_rows[:, rows] = jnp.broadcast_to(weighted * inverse, (8, RB))
            spread = jnp.transpose(jnp.broadcast_to(inverse, (DH, RB)))
            inv_rows[h, rows, :] = spread
            q_scaled[rows, :] = (qn[h, rows, :].astype(F32) * (spread * SCALE)).astype(BF16)
            up_scaled[rows, :] = (up[h, rows, :].astype(F32) * spread).astype(BF16)

        def key_grads(keys, rows):
            gs = (
                expo[keys, rows].astype(F32) * (gprobs[keys, rows] - dot_rows[0:1, rows])
            ).astype(BF16)
            gscores[h, keys, rows] = gs
            return (
                dot(gs, q_scaled[rows, :], NN),
                dot(expo[keys, rows], up_scaled[rows, :], NN),
            )

        def gain_term(grad_kn, keys):
            return fold(grad_kn * keys.astype(F32))

        def root_grads(half_x):
            count = N_ROOT // 2
            keys = slice(half_x * count, (half_x + 1) * count)
            grads = key_grads(keys, slice(0, Q_ROWS))
            gain_part[...] += gain_term(grads[0], kv[h, 0, 0, half_x].reshape(count, DH))
            for t in range(2):
                terms = grads[t].reshape(4, 2, R_DEV, DH).astype(BF16)
                for core in range(2):
                    parts[2 * h, core, half_x, :, t] = terms[:, core]

        def side_grads():
            leaf_rows = slice(LEAF_AT, Q_ROWS)
            grads = key_grads(slice(N_ROOT, N_ROOT + SPAN + L_DEV), leaf_rows)
            gain_part[...] += gain_term(grads[0], side[h, 0, : SPAN + L_DEV, :])
            cols = pl.ds(pl.multiple_of(h * DH, DH), DH)
            rows = slice(R_DEV + B_DEV, ROWS)
            raw = k_ref[rows, cols].astype(F32)
            gk_ref[rows, cols] = norm_backward(
                raw, inverse_norm(raw), kgain_ref[...], grads[0][SPAN:]
            ).astype(BF16)
            gv_ref[rows, cols] = grads[1][SPAN:].astype(BF16)
            own_grads = key_grads(slice(N_ROOT, N_ROOT + SPAN), slice(GQ * R_DEV, LEAF_AT))
            gain_part[...] += gain_term(own_grads[0], side[h, 0, SPAN + L_DEV :, :])
            for b in range(4):
                to_parent = jnp.where(parent == b, 1.0, 0.0)
                to_own = jnp.where(own_branch == b, 1.0, 0.0)
                for t in range(2):
                    both = grads[t][:SPAN] * to_parent + own_grads[t] * to_own
                    for q in range(4):
                        owner = 4 * b + q
                        parts[2 * h + 1, owner % 2, owner // 8, (owner // 2) % 4, t] = both[
                            q * B_DEV : (q + 1) * B_DEV
                        ].astype(BF16)

        for rb in range(3):
            root_scores(rb)
        gather_b(2 * h + 1)
        for rb in range(3, 5):
            root_scores(rb)

        @pl.when(h > 0)
        def _():
            reduce_a(2 * h - 2)
            reduce_a(2 * h - 1)

        gather_c(2 * h + 1)
        pick_side()
        for rb in range(5):
            side_scores(rb)
        for n in range(2):
            root_grads(n)
        r_core(2 * h).start()
        pl.when(h < HK - 1)(lambda: gather_b(2 * h + 2))
        side_grads()
        r_core(2 * h + 1).start()

        @pl.when(h > 1)
        def _():
            reduce_b(2 * h - 4)
            reduce_b(2 * h - 3)

        pl.when(h < HK - 1)(lambda: gather_c(2 * h + 2))
        return carry

    lax.fori_loop(0, HK, one_head, 0)

    def store_q(h):
        cols = pl.ds(h * GQ * DH, GQ * DH)
        return pltpu.make_async_copy(gq_ref.at[:, cols], gq_hbm.at[:, cols], io_sem.at[h])

    def queries_of(h):
        def query_grads(rb):
            rows = slice(rb * RB, (rb + 1) * RB)
            grads = dot(gscores[h, :N_ROOT, rows], kv[h, 0, 0].reshape(N_ROOT, DH), TN)
            if rb == 1:
                grads += dot(gscores[h, N_ROOT : N_ROOT + SPAN, rows], side[h, 0, SPAN + L_DEV :, :], TN)
            if rb >= 2:
                grads += dot(gscores[h, N_ROOT:, rows], side[h, 0, : SPAN + L_DEV, :], TN)
            grad_qn[rows, :] = grads * (inv_rows[h, rows, :] * SCALE)

        def finish_queries():
            for start, count, at in SEGMENTS:
                for g in range(GQ):
                    cols = pl.ds(pl.multiple_of(h * GQ * DH + g * DH, DH), DH)
                    rows = slice(start, start + count)
                    grads = grad_qn[at + g * count : at + (g + 1) * count, :]
                    raw = q_ref[rows, cols].astype(F32)
                    inverse = inverse_norm(raw)
                    gq_ref[rows, cols] = norm_backward(
                        raw, inverse, qgain_ref[...], grads
                    ).astype(BF16)

        for rb in range(5):
            query_grads(rb)
        finish_queries()
        store_q(h).start()

    def a_copy(step, target):
        return pltpu.make_async_remote_copy(
            src_ref=gain_seq.at[0],
            dst_ref=gain_seq.at[step],
            send_sem=a_send.at[step],
            recv_sem=a_recv.at[step],
            device_id=(me_leaf, target),
            device_id_type=MESH,
        )

    def b_copy(step, target):
        return pltpu.make_async_remote_copy(
            src_ref=gain_leaf.at[0],
            dst_ref=gain_leaf.at[step],
            send_sem=b_send.at[step],
            recv_sem=b_recv.at[step],
            device_id=(target, me),
            device_id_type=MESH,
        )

    def a_start(step, carry):
        a_copy(step, (me + step) % N_SEQ).start()
        return carry

    def b_start(step, carry):
        b_copy(step, (me_leaf + step) % n_leaf).start()
        return carry

    def a_wait(step, total):
        a_copy(step, (me + step) % N_SEQ).wait()
        return total + gain_seq[step]

    def b_wait(step, total):
        b_copy(step, (me_leaf + step) % n_leaf).wait()
        return total + gain_leaf[step]

    root, branch = HALVES - 2, HALVES - 1
    gain_seq[0] = gain_part[...]
    lax.fori_loop(1, N_SEQ, a_start, 0)
    reduce_a(root)
    queries_of(0)
    reduce_a(branch)
    queries_of(1)
    gain_leaf[0] = lax.fori_loop(1, N_SEQ, a_wait, gain_seq[0])
    lax.fori_loop(1, n_leaf, b_start, 0)
    reduce_b(root - 2)
    reduce_b(branch - 2)
    queries_of(2)
    queries_of(3)
    reduce_b(root)
    gain = jnp.sum(lax.fori_loop(1, n_leaf, b_wait, gain_leaf[0]), axis=0, keepdims=True)
    row = lax.broadcasted_iota(jnp.int32, (8, DH), 0)
    gains_ref[...] = jnp.where(row == 0, gain / qgain_ref[...], gain / kgain_ref[...])
    reduce_b(branch)
    for half in range(HALVES):
        gather_sent(half)
        reduce_sent(half)
    for h in range(HK):
        store_q(h).wait()


def hand_over(gq_in, gk_in, gv_in, gains_in, gq_out, gk_out, gv_out, qg_out, kg_out, gq, gk, gv, sem):
    pieces = [(gk_in, gk, gk_out), (gv_in, gv, gv_out)]
    step = ROWS // 4
    for n in range(4):
        rows = pl.ds(n * step, step)
        pieces.append((gq_in.at[rows], gq.at[rows], gq_out.at[rows]))
    loads = [pltpu.make_async_copy(p[0], p[1], sem.at[0, n]) for n, p in enumerate(pieces)]
    stores = [pltpu.make_async_copy(p[1], p[2], sem.at[1, n]) for n, p in enumerate(pieces)]
    for load in loads:
        load.start()
    qg_out[...] = gains_in[0:1, :]
    kg_out[...] = gains_in[1:2, :]
    for load, store in zip(loads, stores):
        load.wait()
        store.start()
    for store in stores:
        store.wait()


def on_device(
    query_raw, key_raw, value_raw, grad_out, query_gain, key_gain, leaf_parent, leaf_blocks
):
    n_leaf = lax.axis_size("leaf")
    vmem = pl.BlockSpec(memory_space=pltpu.VMEM)
    smem = pl.BlockSpec(memory_space=pltpu.SMEM)
    hbm = pl.BlockSpec(memory_space=pl.ANY)
    keys = N_ROOT + SPAN + L_DEV
    dma = pltpu.SemaphoreType.DMA
    grad_query, grad_key, grad_value, gains = pl.pallas_call(
        functools.partial(kernel, n_leaf),
        out_shape=(
            jax.ShapeDtypeStruct((ROWS, HQ * DH), BF16),
            jax.ShapeDtypeStruct((ROWS, HK * DH), BF16),
            jax.ShapeDtypeStruct((ROWS, HK * DH), BF16),
            jax.ShapeDtypeStruct((8, DH), F32),
        ),
        in_specs=[smem, smem, hbm, vmem, vmem, hbm, vmem, vmem],
        out_specs=(hbm, vmem, vmem, vmem),
        scratch_shapes=[
            pltpu.VMEM((ROWS, HQ * DH), BF16),
            pltpu.VMEM((ROWS, HQ * DH), BF16),
            pltpu.VMEM((ROWS, HQ * DH), BF16),
            pltpu.VMEM((HK, 2, 2, 2, 4, 2, R_DEV, DH), BF16),
            pltpu.VMEM((HK, 2, L_DEV, DH), BF16),
            pltpu.VMEM((HK, 2, 2 * SPAN + L_DEV, DH), BF16),
            pltpu.VMEM((HK, Q_ROWS, DH), BF16),
            pltpu.VMEM((HK, Q_ROWS, DH), BF16),
            pltpu.VMEM((keys, Q_ROWS), BF16),
            pltpu.VMEM((keys, Q_ROWS), F32),
            pltpu.VMEM((HK, keys, Q_ROWS), BF16),
            pltpu.VMEM((Q_ROWS, DH), BF16),
            pltpu.VMEM((Q_ROWS, DH), BF16),
            pltpu.VMEM((HK, Q_ROWS, DH), F32),
            pltpu.VMEM((8, Q_ROWS), F32),
            pltpu.VMEM((2, 8, Q_ROWS), F32),
            pltpu.VMEM((Q_ROWS, DH), F32),
            pltpu.VMEM((HALVES, 2, 2, 4, 2, R_DEV, DH), BF16),
            pltpu.VMEM((HALVES, 2, 4, 2, R_DEV, DH), BF16),
            pltpu.VMEM((HALVES, CHIPS, 2, R_DEV, DH), BF16),
            pltpu.VMEM((8, DH), F32),
            pltpu.VMEM((N_SEQ, 8, DH), F32),
            pltpu.VMEM((n_leaf, 8, DH), F32),
            dma((HALVES, CHIPS)),
            dma((HALVES, CHIPS)),
            dma((HALVES, CHIPS)),
            dma((HALVES, CHIPS)),
            dma((N_SEQ,)),
            dma((N_SEQ,)),
            dma((n_leaf,)),
            dma((n_leaf,)),
            dma((HK + 2,)),
        ],
        compiler_params=pltpu.CompilerParams(
            collective_id=0, has_side_effects=True, vmem_limit_bytes=60 * 2**20
        ),
        name="attention_backward",
    )(
        leaf_parent,
        leaf_blocks,
        query_raw[0],
        key_raw[0],
        value_raw[0],
        grad_out[0],
        query_gain.reshape(1, DH),
        key_gain.reshape(1, DH),
    )
    grad_query, grad_key, grad_value, query_gain_grad, key_gain_grad = pl.pallas_call(
        hand_over,
        out_shape=(
            jax.ShapeDtypeStruct((ROWS, HQ * DH), BF16),
            jax.ShapeDtypeStruct((ROWS, HK * DH), BF16),
            jax.ShapeDtypeStruct((ROWS, HK * DH), BF16),
            jax.ShapeDtypeStruct((1, DH), F32),
            jax.ShapeDtypeStruct((1, DH), F32),
        ),
        in_specs=[hbm, hbm, hbm, vmem],
        out_specs=(hbm, hbm, hbm, vmem, vmem),
        scratch_shapes=[
            pltpu.VMEM((ROWS, HQ * DH), BF16),
            pltpu.VMEM((ROWS, HK * DH), BF16),
            pltpu.VMEM((ROWS, HK * DH), BF16),
            dma((2, 6)),
        ],
        name="hand_over",
    )(grad_query, grad_key, grad_value, gains)
    return (
        grad_query[None],
        grad_key[None],
        grad_value[None],
        query_gain_grad[0],
        key_gain_grad[0],
    )


def solution(mesh):
    return jax.shard_map(
        on_device,
        mesh=mesh,
        in_specs=(
            P("leaf", "seq", None),
            P("leaf", "seq", None),
            P("leaf", "seq", None),
            P("leaf", "seq", None),
            P(),
            P(),
            P("leaf", "seq"),
            P("leaf", "seq"),
        ),
        out_specs=(
            P("leaf", "seq", None),
            P("leaf", "seq", None),
            P("leaf", "seq", None),
            P(),
            P(),
        ),
        check_vma=False,
    )
```

```python
import functools
import math

import jax
import jax.numpy as jnp
from jax import lax
from jax.experimental import pallas as pl
from jax.experimental.pallas import tpu as pltpu
from jax.sharding import PartitionSpec as P

HQ = 16
HK = 4
DH = 128
GQ = HQ // HK
R_DEV = 64
B_DEV = 64
LEAF_BLOCK = 64
L_DEV = 192
ROWS = 320
N_SEQ = 16
N_ROOT = R_DEV * N_SEQ
SPAN = 256
RB = 256
Q_ROWS = ROWS * GQ
LEAF_AT = GQ * (R_DEV + B_DEV)
EPS = 1e-06
SCALE = 1.0 / math.sqrt(DH)
EXP2_SCALE = SCALE / math.log(2.0)

F32 = jnp.float32
BF16 = jnp.bfloat16
MESH = pl.DeviceIdType.MESH
NT = (((1,), (1,)), ((), ()))
NN = (((1,), (0,)), ((), ()))
TN = (((0,), (0,)), ((), ()))

SEGMENTS = ((0, R_DEV, 0), (R_DEV, B_DEV, GQ * R_DEV), (R_DEV + B_DEV, L_DEV, LEAF_AT))

CHIPS = 8
HALVES = 2 * HK


def dot(left, right, dims):
    return lax.dot_general(left, right, dims, preferred_element_type=F32)


def inverse_norm(values):
    return lax.rsqrt(jnp.mean(values * values, axis=-1, keepdims=True) + EPS)


def norm_backward(values, inverse, gain, upstream):
    scaled = upstream * gain
    mean = jnp.mean(scaled * values, axis=-1, keepdims=True)
    return inverse * scaled - values * (inverse * inverse * inverse * mean)


def fold(array):
    return jnp.sum(array.reshape(array.shape[0] // 8, 8, array.shape[1]), axis=0)


def kernel(
    n_leaf,
    parent_ref,
    blocks_ref,
    q_hbm,
    k_ref,
    v_ref,
    u_hbm,
    qgain_ref,
    kgain_ref,
    gq_hbm,
    gk_ref,
    gv_ref,
    gains_ref,
    q_ref,
    u_ref,
    gq_ref,
    kv,
    leaf_kv,
    side,
    qn,
    up,
    expo,
    gprobs,
    gscores,
    q_scaled,
    up_scaled,
    inv_rows,
    dot_rows,
    sums,
    grad_qn,
    parts,
    from_core,
    from_chip,
    gain_part,
    gain_seq,
    gain_leaf,
    g_send,
    g_recv,
    r_send,
    r_recv,
    a_send,
    a_recv,
    b_send,
    b_recv,
    io_sem,
):
    me = lax.axis_index("seq")
    me_leaf = lax.axis_index("leaf")
    x = me // 8
    y = (me // 2) % 4
    c = me % 2
    def place(px, py, pc):
        return px * 8 + py * 2 + pc

    dev_core = place(x, y, 1 - c)
    parent = parent_ref[0, 0]
    leaf_length = blocks_ref[0, 0] * LEAF_BLOCK
    own_branch = me // 4

    load_q = pltpu.make_async_copy(q_hbm, q_ref, io_sem.at[HK])
    load_u = pltpu.make_async_copy(u_hbm, u_ref, io_sem.at[HK + 1])

    barrier = pltpu.get_barrier_semaphore()

    def greet_seq(step, carry):
        pl.semaphore_signal(
            barrier, inc=1, device_id=(me_leaf, (me + step) % N_SEQ), device_id_type=MESH
        )
        return carry

    def greet_leaf(step, carry):
        pl.semaphore_signal(
            barrier, inc=1, device_id=((me_leaf + step) % n_leaf, me), device_id_type=MESH
        )
        return carry

    lax.fori_loop(1, N_SEQ, greet_seq, 0)
    lax.fori_loop(1, n_leaf, greet_leaf, 0)

    load_q.start()
    load_u.start()


    def prepare_keys(h):
        cols = slice(h * DH, (h + 1) * DH)
        raw = k_ref[:, cols].astype(F32)
        normed = (raw * inverse_norm(raw) * kgain_ref[...]).astype(BF16)
        values = v_ref[:, cols]
        kv[h, 0, 0, x, y, c] = normed[:R_DEV]
        kv[h, 1, 0, x, y, c] = normed[R_DEV : R_DEV + B_DEV]
        leaf_kv[h, 0] = normed[R_DEV + B_DEV :]
        kv[h, 0, 1, x, y, c] = values[:R_DEV]
        kv[h, 1, 1, x, y, c] = values[R_DEV : R_DEV + B_DEV]
        leaf_kv[h, 1] = values[R_DEV + B_DEV :]

    prepare_keys(0)
    pl.semaphore_wait(barrier, N_SEQ - 1 + n_leaf - 1)

    def chip_at(number, sign):
        other = number // 4
        return x + other * (1 - 2 * x), (y + sign * (number % 4)) % 4

    def g_copy(half, number, px, py, target):
        ref = kv.at[half // 2, half % 2, :, px, py, c]
        return pltpu.make_async_remote_copy(
            src_ref=ref,
            dst_ref=ref,
            send_sem=g_send.at[half, number],
            recv_sem=g_recv.at[half, number],
            device_id=(me_leaf, target),
            device_id_type=MESH,
        )

    def g_core(half, core):
        ref = kv.at[half // 2, half % 2, :, :, :, core]
        return pltpu.make_async_remote_copy(
            src_ref=ref,
            dst_ref=ref,
            send_sem=g_send.at[half, 0],
            recv_sem=g_recv.at[half, 0],
            device_id=(me_leaf, dev_core),
            device_id_type=MESH,
        )

    def gather_a(half):
        for number in range(1, CHIPS):
            px, py = chip_at(number, 1)
            g_copy(half, number, x, y, place(px, py, c)).start()

    def gather_b(half):
        for number in range(1, CHIPS):
            px, py = chip_at(number, 3)
            g_copy(half, number, px, py, place(px, py, c)).wait_recv()
        g_core(half, c).start()

    def gather_c(half):
        g_core(half, 1 - c).wait_recv()

    def gather_sent(half):
        for number in range(1, CHIPS):
            px, py = chip_at(number, 1)
            g_copy(half, number, x, y, place(px, py, c)).wait_send()
        g_core(half, c).wait_send()

    def r_core(half):
        return pltpu.make_async_remote_copy(
            src_ref=parts.at[half, 1 - c],
            dst_ref=from_core.at[half],
            send_sem=r_send.at[half, 0],
            recv_sem=r_recv.at[half, 0],
            device_id=(me_leaf, dev_core),
            device_id_type=MESH,
        )

    def r_copy(half, number):
        px, py = chip_at(number, 1)
        return pltpu.make_async_remote_copy(
            src_ref=parts.at[half, c, px, py],
            dst_ref=from_chip.at[half, number],
            send_sem=r_send.at[half, number],
            recv_sem=r_recv.at[half, number],
            device_id=(me_leaf, place(px, py, c)),
            device_id_type=MESH,
        )

    def reduce_a(half):
        r_core(half).wait_recv()
        for px in range(2):
            for py in range(4):
                parts[half, c, px, py] = (
                    parts[half, c, px, py].astype(F32) + from_core[half, px, py].astype(F32)
                ).astype(BF16)
        for number in range(1, CHIPS):
            r_copy(half, number).start()

    def reduce_b(half):
        for number in range(1, CHIPS):
            r_copy(half, number).wait_recv()
        total = parts[half, c, x, y].astype(F32)
        for number in range(1, CHIPS):
            total += from_chip[half, number].astype(F32)
        cols = pl.ds(pl.multiple_of((half // 2) * DH, DH), DH)
        rows = pl.ds(pl.multiple_of((half % 2) * R_DEV, R_DEV), R_DEV)
        raw = k_ref[rows, cols].astype(F32)
        gk_ref[rows, cols] = norm_backward(
            raw, inverse_norm(raw), kgain_ref[...], total[0]
        ).astype(BF16)
        gv_ref[rows, cols] = total[1].astype(BF16)

    def reduce_sent(half):
        r_core(half).wait_send()
        for number in range(1, CHIPS):
            r_copy(half, number).wait_send()

    def prepare(h):
        for start, count, at in SEGMENTS:
            for g in range(GQ):
                cols = pl.ds(pl.multiple_of(h * GQ * DH + g * DH, DH), DH)
                rows = slice(start, start + count)
                dst = slice(at + g * count, at + (g + 1) * count)
                raw = q_ref[rows, cols].astype(F32)
                qn[h, dst, :] = (raw * inverse_norm(raw) * qgain_ref[...]).astype(BF16)
                grads = u_ref[rows, cols]
                if start == R_DEV + B_DEV:
                    ids = lax.broadcasted_iota(jnp.int32, (count, DH), 0)
                    grads = jnp.where(ids < leaf_length, grads.astype(F32), 0.0).astype(BF16)
                up[h, dst, :] = grads

    for half in range(2):
        gather_a(half)
    for h in range(1, HK):
        prepare_keys(h)
    for half in range(2, HALVES):
        gather_a(half)
    load_q.wait()
    load_u.wait()
    prepare(0)
    prepare(1)
    prepare(2)
    gather_b(0)
    prepare(3)
    gather_c(0)
    gain_part[...] = jnp.zeros_like(gain_part)

    def one_head(h, carry):
        def pick_side():
            for t in range(2):
                picked = kv[h, 1, t, 0, 0:2].reshape(SPAN, DH)
                for b in range(1, 4):
                    picked = lax.select_n(
                        parent == b,
                        picked,
                        kv[h, 1, t, b // 2, b % 2 * 2 : b % 2 * 2 + 2].reshape(SPAN, DH),
                    )
                side[h, t, 0:SPAN, :] = picked
                side[h, t, SPAN : SPAN + L_DEV, :] = leaf_kv[h, t]
                side[h, t, SPAN + L_DEV :, :] = kv[h, 1, t, x, pl.ds(y // 2 * 2, 2)].reshape(
                    SPAN, DH
                )

        def key_ids(count):
            return lax.broadcasted_iota(jnp.int32, (count, RB), 0)

        def row_ids(count, first, period):
            return (lax.broadcasted_iota(jnp.int32, (count, RB), 1) + first) % period

        def chunk(rb, keys, values, dst, allowed):
            rows = slice(rb * RB, (rb + 1) * RB)
            count = keys.shape[0]
            e = jnp.exp2(dot(keys, qn[h, rows, :], NT) * EXP2_SCALE)
            if allowed is not None:
                e = jnp.where(allowed, e, 0.0)
            gp = dot(values, up[h, rows, :], NT)
            expo[dst : dst + count, rows] = e.astype(BF16)
            gprobs[dst : dst + count, rows] = gp
            return fold(e), fold(e * gp)

        def root_block(t, n):
            return kv[h, 0, t, n // 2, n % 2 * 2 : n % 2 * 2 + 2].reshape(SPAN, DH)

        def root_scores(rb):
            found = []
            for n in range(N_ROOT // SPAN):
                allowed = None
                if rb == 0:
                    allowed = key_ids(SPAN) + n * SPAN <= row_ids(SPAN, 0, R_DEV) + me * R_DEV
                found.append(chunk(rb, root_block(0, n), root_block(1, n), n * SPAN, allowed))
            rows = slice(rb * RB, (rb + 1) * RB)
            sums[0, :, rows] = sum(f[0] for f in found)
            sums[1, :, rows] = sum(f[1] for f in found)

        def side_scores(rb):
            rows = slice(rb * RB, (rb + 1) * RB)
            found = [(sums[0, :, rows], sums[1, :, rows])]
            if rb == 1:
                allowed = key_ids(SPAN) <= row_ids(SPAN, 0, B_DEV) + (me % 4) * B_DEV
                keys = slice(SPAN + L_DEV, 2 * SPAN + L_DEV)
                found.append(chunk(rb, side[h, 0, keys, :], side[h, 1, keys, :], N_ROOT, allowed))
            if rb >= 2:
                found.append(
                    chunk(rb, side[h, 0, :SPAN, :], side[h, 1, :SPAN, :], N_ROOT, None)
                )
                ids = key_ids(L_DEV)
                allowed = (ids <= row_ids(L_DEV, (rb - 2) * RB, L_DEV)) & (ids < leaf_length)
                keys = slice(SPAN, SPAN + L_DEV)
                found.append(
                    chunk(rb, side[h, 0, keys, :], side[h, 1, keys, :], N_ROOT + SPAN, allowed)
                )
            total = jnp.sum(sum(f[0] for f in found), axis=0, keepdims=True)
            weighted = jnp.sum(sum(f[1] for f in found), axis=0, keepdims=True)
            inverse = 1.0 / total
            dot_rows[:, rows] = jnp.broadcast_to(weighted * inverse, (8, RB))
            spread = jnp.transpose(jnp.broadcast_to(inverse, (DH, RB)))
            inv_rows[h, rows, :] = spread
            q_scaled[rows, :] = (qn[h, rows, :].astype(F32) * (spread * SCALE)).astype(BF16)
            up_scaled[rows, :] = (up[h, rows, :].astype(F32) * spread).astype(BF16)

        def key_grads(keys, rows):
            gs = (
                expo[keys, rows].astype(F32) * (gprobs[keys, rows] - dot_rows[0:1, rows])
            ).astype(BF16)
            gscores[h, keys, rows] = gs
            return (
                dot(gs, q_scaled[rows, :], NN),
                dot(expo[keys, rows], up_scaled[rows, :], NN),
            )

        def gain_term(grad_kn, keys):
            return fold(grad_kn * keys.astype(F32))

        def root_grads(half_x):
            count = N_ROOT // 2
            keys = slice(half_x * count, (half_x + 1) * count)
            grads = key_grads(keys, slice(0, Q_ROWS))
            gain_part[...] += gain_term(grads[0], kv[h, 0, 0, half_x].reshape(count, DH))
            for t in range(2):
                terms = grads[t].reshape(4, 2, R_DEV, DH).astype(BF16)
                for core in range(2):
                    parts[2 * h, core, half_x, :, t] = terms[:, core]

        def side_grads():
            leaf_rows = slice(LEAF_AT, Q_ROWS)
            grads = key_grads(slice(N_ROOT, N_ROOT + SPAN + L_DEV), leaf_rows)
            gain_part[...] += gain_term(grads[0], side[h, 0, : SPAN + L_DEV, :])
            cols = pl.ds(pl.multiple_of(h * DH, DH), DH)
            rows = slice(R_DEV + B_DEV, ROWS)
            raw = k_ref[rows, cols].astype(F32)
            gk_ref[rows, cols] = norm_backward(
                raw, inverse_norm(raw), kgain_ref[...], grads[0][SPAN:]
            ).astype(BF16)
            gv_ref[rows, cols] = grads[1][SPAN:].astype(BF16)
            own_grads = key_grads(slice(N_ROOT, N_ROOT + SPAN), slice(GQ * R_DEV, LEAF_AT))
            gain_part[...] += gain_term(own_grads[0], side[h, 0, SPAN + L_DEV :, :])
            for b in range(4):
                to_parent = jnp.where(parent == b, 1.0, 0.0)
                to_own = jnp.where(own_branch == b, 1.0, 0.0)
                for t in range(2):
                    both = grads[t][:SPAN] * to_parent + own_grads[t] * to_own
                    for q in range(4):
                        owner = 4 * b + q
                        parts[2 * h + 1, owner % 2, owner // 8, (owner // 2) % 4, t] = both[
                            q * B_DEV : (q + 1) * B_DEV
                        ].astype(BF16)

        root_scores(0)
        pl.when(h > 0)(lambda: reduce_a(2 * h - 2))
        for rb in range(1, 3):
            root_scores(rb)
        gather_b(2 * h + 1)
        pl.when(h > 0)(lambda: reduce_a(2 * h - 1))
        for rb in range(3, 5):
            root_scores(rb)
        gather_c(2 * h + 1)
        pick_side()
        for rb in range(5):
            side_scores(rb)
        for n in range(2):
            root_grads(n)
        r_core(2 * h).start()
        pl.when(h < HK - 1)(lambda: gather_b(2 * h + 2))
        side_grads()
        r_core(2 * h + 1).start()

        @pl.when(h > 1)
        def _():
            reduce_b(2 * h - 4)
            reduce_b(2 * h - 3)

        pl.when(h < HK - 1)(lambda: gather_c(2 * h + 2))
        return carry

    lax.fori_loop(0, HK, one_head, 0)

    def store_q(h):
        cols = pl.ds(h * GQ * DH, GQ * DH)
        return pltpu.make_async_copy(gq_ref.at[:, cols], gq_hbm.at[:, cols], io_sem.at[h])

    def queries_of(h):
        def query_grads(rb):
            rows = slice(rb * RB, (rb + 1) * RB)
            grads = dot(gscores[h, :N_ROOT, rows], kv[h, 0, 0].reshape(N_ROOT, DH), TN)
            if rb == 1:
                grads += dot(gscores[h, N_ROOT : N_ROOT + SPAN, rows], side[h, 0, SPAN + L_DEV :, :], TN)
            if rb >= 2:
                grads += dot(gscores[h, N_ROOT:, rows], side[h, 0, : SPAN + L_DEV, :], TN)
            grad_qn[rows, :] = grads * (inv_rows[h, rows, :] * SCALE)

        def finish_queries():
            for start, count, at in SEGMENTS:
                for g in range(GQ):
                    cols = pl.ds(pl.multiple_of(h * GQ * DH + g * DH, DH), DH)
                    rows = slice(start, start + count)
                    grads = grad_qn[at + g * count : at + (g + 1) * count, :]
                    raw = q_ref[rows, cols].astype(F32)
                    inverse = inverse_norm(raw)
                    gq_ref[rows, cols] = norm_backward(
                        raw, inverse, qgain_ref[...], grads
                    ).astype(BF16)

        for rb in range(5):
            query_grads(rb)
        finish_queries()
        store_q(h).start()

    def a_copy(step, target):
        return pltpu.make_async_remote_copy(
            src_ref=gain_seq.at[0],
            dst_ref=gain_seq.at[step],
            send_sem=a_send.at[step],
            recv_sem=a_recv.at[step],
            device_id=(me_leaf, target),
            device_id_type=MESH,
        )

    def b_copy(step, target):
        return pltpu.make_async_remote_copy(
            src_ref=gain_leaf.at[0],
            dst_ref=gain_leaf.at[step],
            send_sem=b_send.at[step],
            recv_sem=b_recv.at[step],
            device_id=(target, me),
            device_id_type=MESH,
        )

    def a_start(step, carry):
        a_copy(step, (me + step) % N_SEQ).start()
        return carry

    def b_start(step, carry):
        b_copy(step, (me_leaf + step) % n_leaf).start()
        return carry

    def a_wait(step, total):
        a_copy(step, (me + step) % N_SEQ).wait()
        return total + gain_seq[step]

    def b_wait(step, total):
        b_copy(step, (me_leaf + step) % n_leaf).wait()
        return total + gain_leaf[step]

    root, branch = HALVES - 2, HALVES - 1
    gain_seq[0] = gain_part[...]
    lax.fori_loop(1, N_SEQ, a_start, 0)
    reduce_a(root)
    queries_of(0)
    reduce_a(branch)
    queries_of(1)
    gain_leaf[0] = lax.fori_loop(1, N_SEQ, a_wait, gain_seq[0])
    lax.fori_loop(1, n_leaf, b_start, 0)
    queries_of(2)
    queries_of(3)
    reduce_b(root - 2)
    reduce_b(branch - 2)
    reduce_b(root)
    gain = jnp.sum(lax.fori_loop(1, n_leaf, b_wait, gain_leaf[0]), axis=0, keepdims=True)
    row = lax.broadcasted_iota(jnp.int32, (8, DH), 0)
    gains_ref[...] = jnp.where(row == 0, gain / qgain_ref[...], gain / kgain_ref[...])
    reduce_b(branch)
    for half in range(HALVES):
        gather_sent(half)
        reduce_sent(half)
    for h in range(HK):
        store_q(h).wait()


def hand_over(gq_in, gk_in, gv_in, gains_in, gq_out, gk_out, gv_out, qg_out, kg_out, gq, gk, gv, sem):
    pieces = [(gk_in, gk, gk_out), (gv_in, gv, gv_out)]
    step = ROWS // 4
    for n in range(4):
        rows = pl.ds(n * step, step)
        pieces.append((gq_in.at[rows], gq.at[rows], gq_out.at[rows]))
    loads = [pltpu.make_async_copy(p[0], p[1], sem.at[0, n]) for n, p in enumerate(pieces)]
    stores = [pltpu.make_async_copy(p[1], p[2], sem.at[1, n]) for n, p in enumerate(pieces)]
    for load in loads:
        load.start()
    qg_out[...] = gains_in[0:1, :]
    kg_out[...] = gains_in[1:2, :]
    for load, store in zip(loads, stores):
        load.wait()
        store.start()
    for store in stores:
        store.wait()


def on_device(
    query_raw, key_raw, value_raw, grad_out, query_gain, key_gain, leaf_parent, leaf_blocks
):
    n_leaf = lax.axis_size("leaf")
    vmem = pl.BlockSpec(memory_space=pltpu.VMEM)
    smem = pl.BlockSpec(memory_space=pltpu.SMEM)
    hbm = pl.BlockSpec(memory_space=pl.ANY)
    keys = N_ROOT + SPAN + L_DEV
    dma = pltpu.SemaphoreType.DMA
    grad_query, grad_key, grad_value, gains = pl.pallas_call(
        functools.partial(kernel, n_leaf),
        out_shape=(
            jax.ShapeDtypeStruct((ROWS, HQ * DH), BF16),
            jax.ShapeDtypeStruct((ROWS, HK * DH), BF16),
            jax.ShapeDtypeStruct((ROWS, HK * DH), BF16),
            jax.ShapeDtypeStruct((8, DH), F32),
        ),
        in_specs=[smem, smem, hbm, vmem, vmem, hbm, vmem, vmem],
        out_specs=(hbm, vmem, vmem, vmem),
        scratch_shapes=[
            pltpu.VMEM((ROWS, HQ * DH), BF16),
            pltpu.VMEM((ROWS, HQ * DH), BF16),
            pltpu.VMEM((ROWS, HQ * DH), BF16),
            pltpu.VMEM((HK, 2, 2, 2, 4, 2, R_DEV, DH), BF16),
            pltpu.VMEM((HK, 2, L_DEV, DH), BF16),
            pltpu.VMEM((HK, 2, 2 * SPAN + L_DEV, DH), BF16),
            pltpu.VMEM((HK, Q_ROWS, DH), BF16),
            pltpu.VMEM((HK, Q_ROWS, DH), BF16),
            pltpu.VMEM((keys, Q_ROWS), BF16),
            pltpu.VMEM((keys, Q_ROWS), F32),
            pltpu.VMEM((HK, keys, Q_ROWS), BF16),
            pltpu.VMEM((Q_ROWS, DH), BF16),
            pltpu.VMEM((Q_ROWS, DH), BF16),
            pltpu.VMEM((HK, Q_ROWS, DH), F32),
            pltpu.VMEM((8, Q_ROWS), F32),
            pltpu.VMEM((2, 8, Q_ROWS), F32),
            pltpu.VMEM((Q_ROWS, DH), F32),
            pltpu.VMEM((HALVES, 2, 2, 4, 2, R_DEV, DH), BF16),
            pltpu.VMEM((HALVES, 2, 4, 2, R_DEV, DH), BF16),
            pltpu.VMEM((HALVES, CHIPS, 2, R_DEV, DH), BF16),
            pltpu.VMEM((8, DH), F32),
            pltpu.VMEM((N_SEQ, 8, DH), F32),
            pltpu.VMEM((n_leaf, 8, DH), F32),
            dma((HALVES, CHIPS)),
            dma((HALVES, CHIPS)),
            dma((HALVES, CHIPS)),
            dma((HALVES, CHIPS)),
            dma((N_SEQ,)),
            dma((N_SEQ,)),
            dma((n_leaf,)),
            dma((n_leaf,)),
            dma((HK + 2,)),
        ],
        compiler_params=pltpu.CompilerParams(
            collective_id=0, has_side_effects=True, vmem_limit_bytes=60 * 2**20
        ),
        name="attention_backward",
    )(
        leaf_parent,
        leaf_blocks,
        query_raw[0],
        key_raw[0],
        value_raw[0],
        grad_out[0],
        query_gain.reshape(1, DH),
        key_gain.reshape(1, DH),
    )
    grad_query, grad_key, grad_value, query_gain_grad, key_gain_grad = pl.pallas_call(
        hand_over,
        out_shape=(
            jax.ShapeDtypeStruct((ROWS, HQ * DH), BF16),
            jax.ShapeDtypeStruct((ROWS, HK * DH), BF16),
            jax.ShapeDtypeStruct((ROWS, HK * DH), BF16),
            jax.ShapeDtypeStruct((1, DH), F32),
            jax.ShapeDtypeStruct((1, DH), F32),
        ),
        in_specs=[hbm, hbm, hbm, vmem],
        out_specs=(hbm, hbm, hbm, vmem, vmem),
        scratch_shapes=[
            pltpu.VMEM((ROWS, HQ * DH), BF16),
            pltpu.VMEM((ROWS, HK * DH), BF16),
            pltpu.VMEM((ROWS, HK * DH), BF16),
            dma((2, 6)),
        ],
        name="hand_over",
    )(grad_query, grad_key, grad_value, gains)
    return (
        grad_query[None],
        grad_key[None],
        grad_value[None],
        query_gain_grad[0],
        key_gain_grad[0],
    )


def solution(mesh):
    return jax.shard_map(
        on_device,
        mesh=mesh,
        in_specs=(
            P("leaf", "seq", None),
            P("leaf", "seq", None),
            P("leaf", "seq", None),
            P("leaf", "seq", None),
            P(),
            P(),
            P("leaf", "seq"),
            P("leaf", "seq"),
        ),
        out_specs=(
            P("leaf", "seq", None),
            P("leaf", "seq", None),
            P("leaf", "seq", None),
            P(),
            P(),
        ),
        check_vma=False,
    )
```
